256 devices in a mesh: ctx: 64 (over y, z_lo, x), head: 4 (over z_hi, core).
Axes of the slice: x: 4, y: 4, z: 8 (z_hi: 2, z_lo: 4; z = z_hi * 4 + z_lo), core: 2. Of those that a mesh axis runs over, the one named last changes fastest.
Arguments:
- queries: bfloat16 [16384, 8192], P('ctx', 'head'), may hold values from -1.78125 to 1.78125
- key_rows: bfloat16 [16384, 8192], P('ctx', 'head'), may hold values from -1.78125 to 1.78125
- value_rows: bfloat16 [16384, 8192], P('ctx', 'head'), may hold values from -18 to 18
- cotangent: bfloat16 [16384, 8192], P('ctx', 'head'), may hold values from -6 to 6
- log_decay: float32 [64, 16384], P('head', 'ctx'), may hold values from -0.6 to 0, as said below
- norm_gain: float32 [8192], P('head'), may hold values from 0.25 to 1.75
Outputs:
- grad_queries: bfloat16 [16384, 8192], P('ctx', 'head')
- grad_keys: bfloat16 [16384, 8192], P('ctx', 'head')
- grad_values: bfloat16 [16384, 8192], P('ctx', 'head')
The draws below stay inside these ranges and needn't reach their ends.
Inputs may be any that keep to these rules, and one draw needn't show every extreme that they name: `log_decay`: per-position logarithm of each head's decay.
All inputs are finite; a program needn't handle non-finite values.
Results may differ from the reference program's by a relative error of at most 0.007.
Values sent between devices are 32-bit elements; how exact they have to be, the bound alone decides.
A program may use at most 320 MiB of HBM per device.

```python
import jax
import jax.numpy as jnp
from jax import lax

HEAD_COUNT = 64
DH = 128
TOK_DEV = 256
SEQUENCE_TOKENS = 16384
FEAT = 8192
N_CTX = 64


def draw_value_rows(key, part):
    key = jax.random.fold_in(key, 23)
    first_key, second_key = jax.random.split(key, 2)
    ramp = jnp.arange(HEAD_COUNT, dtype=jnp.float32) / (HEAD_COUNT - 1)
    head_scale = jnp.exp(jnp.log(3.0) * ramp) * jax.random.uniform(first_key, (HEAD_COUNT,), jnp.float32, 0.8, 1.2)
    column_scale = jnp.repeat(head_scale, DH)
    base_draw = jnp.clip(jax.random.normal(second_key, (SEQUENCE_TOKENS, HEAD_COUNT * DH), jnp.float32), -5.0, 5.0)
    return (base_draw * column_scale[None, :]).astype(jnp.bfloat16)


def draw_log_decay(key, part):
    key = jax.random.fold_in(key, 11)
    random_key_list = jax.random.split(key, 7)
    fast_share = 0.5
    fast_heads = jax.random.uniform(random_key_list[0], (HEAD_COUNT, 1), jnp.float32) < fast_share
    fast_rate = jax.random.uniform(random_key_list[1], (HEAD_COUNT, 1), jnp.float32, 1.0 / 50.0, 1.0 / 30.0)
    slow_rate = jax.random.uniform(random_key_list[2], (HEAD_COUNT, 1), jnp.float32, 0.2, 0.8) / SEQUENCE_TOKENS
    baseline_decay_rate = jnp.where(fast_heads, fast_rate, slow_rate)
    block_total = SEQUENCE_TOKENS // TOK_DEV
    block_multiplier = jnp.exp(jax.random.uniform(random_key_list[3], (HEAD_COUNT, block_total, 1), jnp.float32, jnp.log(0.6), jnp.log(1.6)))
    block_multiplier = jnp.broadcast_to(block_multiplier, (HEAD_COUNT, block_total, TOK_DEV)).reshape(HEAD_COUNT, SEQUENCE_TOKENS)
    noise_amplitude = jax.random.uniform(random_key_list[4], (HEAD_COUNT, SEQUENCE_TOKENS), jnp.float32, 0.5, 1.5)
    spike_locations = jax.random.randint(random_key_list[5], (HEAD_COUNT, 2, 1), 0, SEQUENCE_TOKENS)
    spike_depth = jax.random.uniform(random_key_list[6], (HEAD_COUNT, 2, 1), jnp.float32, 0.22, 0.4)
    token_position_index = jnp.arange(SEQUENCE_TOKENS, dtype=jnp.int32)[None, None, :]
    spike_events = jnp.sum(jnp.where(spike_locations == token_position_index, spike_depth, 0.0), axis=1)
    return -(baseline_decay_rate * block_multiplier * noise_amplitude + spike_events)


def shard_levels(rng, extent, cuts, least, largest):
    def one(position, shards_of):
        draws = jax.random.uniform(jax.random.fold_in(jax.random.fold_in(rng, 6), position), (shards_of,), jnp.float32, least / len(cuts), largest / len(cuts))
        return jnp.repeat(jnp.exp(draws), extent[position] // shards_of).reshape((-1,) + (1,) * (len(extent) - position - 1))

    level = one(*cuts[0])
    for cut in cuts[1:]:
        level = level * one(*cut)
    return level


def bell_draw(rng, extent, deviation, bound, pieces=(), held_as=jnp.bfloat16):
    factor_of = shard_levels(rng, extent, pieces, -0.22, 0.18) if pieces else 1.0
    entries = jax.random.normal(rng, extent, jnp.float32) * deviation * factor_of
    return jnp.minimum(jnp.maximum(entries, -bound), bound).astype(held_as)


def setup_inputs(seed: int = 0) -> dict:
    keys = jax.random.split(jax.random.key(seed), 7)
    queries = bell_draw(keys[0], (SEQUENCE_TOKENS, FEAT), (DH ** -0.25), 1.78125, ((0, 64), (1, 4)))
    key_rows = bell_draw(keys[1], (SEQUENCE_TOKENS, FEAT), (DH ** -0.25), 1.78125, ((0, 64), (1, 4)))
    value_rows = draw_value_rows(jax.random.fold_in(keys[6], 71), 0)
    cotangent = bell_draw(keys[3], (SEQUENCE_TOKENS, FEAT), 1.0, 6.0, ((0, 64), (1, 4)))
    log_decay = draw_log_decay(jax.random.fold_in(keys[6], 71), 0)
    norm_gain = jnp.clip(1.0 + 0.15 * jax.random.normal(keys[5], (FEAT,), jnp.float32), 0.25, 1.75)
    return dict(queries=queries, key_rows=key_rows, value_rows=value_rows, cotangent=cotangent, log_decay=log_decay, norm_gain=norm_gain)


eps_norm = 1e-06

def rounded(array):
    return lax.optimization_barrier(array.astype(jnp.bfloat16)).astype(jnp.float32)

def mixed(pattern, left_side, right_side):
    return jnp.einsum(pattern, left_side, right_side, precision=lax.Precision.HIGHEST)

def causal_decay(cumulative):
    row_count = cumulative.shape[1]
    row_index = lax.broadcasted_iota(jnp.int32, (row_count, row_count), 0)
    col_index = lax.broadcasted_iota(jnp.int32, (row_count, row_count), 1)
    lower_mask = (row_index >= col_index)[None]
    spread = cumulative[:, :, None] - cumulative[:, None, :]
    return jnp.where(lower_mask, jnp.exp(jnp.where(lower_mask, spread, 0.0)), 0.0)

def block_setup(query_blk, key_blk, log_blk):
    cumulative = jnp.cumsum(log_blk, axis=1)
    ending = cumulative[:, -1:]
    forward_gain = jnp.exp(cumulative).T[:, :, None]
    backward_gain = jnp.exp(ending - cumulative).T[:, :, None]
    decay_mask = causal_decay(cumulative)
    scores_fwd = rounded(mixed('thd,jhd->htj', query_blk, key_blk) * decay_mask)
    return (cumulative, forward_gain, backward_gain, decay_mask, scores_fwd)

def reference(queries, key_rows, value_rows, cotangent, log_decay, norm_gain):
    features = HEAD_COUNT * DH

    def blocked(array):
        return array.reshape(N_CTX, TOK_DEV, HEAD_COUNT, DH)
    decay_blocks = log_decay.reshape(HEAD_COUNT, N_CTX, TOK_DEV).transpose(1, 0, 2)

    def forward_step(carried, block_data):
        query_blk, key_blk, value_blk, cot_blk, log_blk = block_data
        query_blk = query_blk.astype(jnp.float32)
        key_blk = key_blk.astype(jnp.float32)
        value_blk = value_blk.astype(jnp.float32)
        cot_blk = cot_blk.astype(jnp.float32)
        cumulative, forward_gain, backward_gain, decay_mask, scores_fwd = block_setup(query_blk, key_blk, log_blk)
        key_weight = rounded(key_blk * backward_gain)
        query_weight = rounded(query_blk * forward_gain)
        block_state = mixed('thd,the->hde', key_weight, value_blk)
        entry_low = rounded(carried)
        output_f = mixed('htj,jhe->the', scores_fwd, value_blk) + mixed('thd,hde->the', query_weight, entry_low)
        flat_out = output_f.reshape(TOK_DEV, features)
        scaled = norm_gain * cot_blk.reshape(TOK_DEV, features)
        root_mean = jnp.sqrt(lax.optimization_barrier(jnp.sum(flat_out * flat_out, axis=1)) / features + eps_norm)
        inner_sum = lax.optimization_barrier(jnp.sum(flat_out * scaled, axis=1))
        d_out = rounded(scaled / root_mean[:, None] - flat_out * (inner_sum / (features * root_mean ** 3))[:, None])
        d_out = d_out.reshape(TOK_DEV, HEAD_COUNT, DH)
        back_scores = rounded(mixed('thd,jhd->htj', d_out, value_blk) * decay_mask)
        dout_weight = rounded(d_out * forward_gain)
        grad_q = mixed('htj,jhd->thd', back_scores, key_blk) + mixed('the,hde->thd', dout_weight, entry_low)
        fall = jnp.exp(cumulative[:, -1])
        following = fall[:, None, None] * carried + block_state
        return (following, (d_out.astype(jnp.bfloat16), grad_q.astype(jnp.bfloat16)))
    start_state = jnp.zeros((HEAD_COUNT, DH, DH), jnp.float32)
    forward_inputs = (blocked(queries), blocked(key_rows), blocked(value_rows), blocked(cotangent), decay_blocks)
    unused, (d_out_all, grad_q_all) = lax.scan(forward_step, start_state, forward_inputs)

    def backward_step(carried, block_data):
        query_blk, key_blk, value_blk, dout_blk, log_blk = block_data
        query_blk = query_blk.astype(jnp.float32)
        key_blk = key_blk.astype(jnp.float32)
        value_blk = value_blk.astype(jnp.float32)
        dout_blk = dout_blk.astype(jnp.float32)
        cumulative, forward_gain, backward_gain, decay_mask, scores_fwd = block_setup(query_blk, key_blk, log_blk)
        key_weight = rounded(key_blk * backward_gain)
        value_weight = rounded(value_blk * backward_gain)
        query_weight = rounded(query_blk * forward_gain)
        back_scores = rounded(mixed('thd,jhd->htj', dout_blk, value_blk) * decay_mask)
        exit_low = rounded(carried)
        grad_k = mixed('hjt,jhd->thd', back_scores, query_blk) + mixed('the,hde->thd', value_weight, exit_low)
        grad_v = mixed('hjt,jhe->the', scores_fwd, dout_blk) + mixed('thd,hde->the', key_weight, exit_low)
        block_grad = mixed('thd,the->hde', query_weight, dout_blk)
        fall = jnp.exp(cumulative[:, -1])
        earlier = block_grad + fall[:, None, None] * carried
        return (earlier, (grad_k.astype(jnp.bfloat16), grad_v.astype(jnp.bfloat16)))
    backward_inputs = (blocked(queries), blocked(key_rows), blocked(value_rows), d_out_all, decay_blocks)
    unused_end, (grad_k_all, grad_v_all) = lax.scan(backward_step, start_state, backward_inputs, reverse=True)
    return (grad_q_all.reshape(SEQUENCE_TOKENS, features), grad_k_all.reshape(SEQUENCE_TOKENS, features), grad_v_all.reshape(SEQUENCE_TOKENS, features))
```

```python
import functools
import itertools

import jax
import jax.numpy as jnp
from jax import lax
from jax.experimental import pallas as pl
from jax.experimental.pallas import tpu as pltpu
from jax.sharding import PartitionSpec as P

eps_norm = 1e-06
MESH = pl.DeviceIdType.MESH
F32, BF16 = jnp.float32, jnp.bfloat16
DH = 128
PARTS = {64: (4, 4, 4), 8: (2, 2, 2)}
X_OUT, Z_OUT, Y_ALL, Z_BACK, X_BACK = range(5)


def nn(a, b, **kw):
    return lax.dot_general(a, b, (((1,), (0,)), ((), ())), preferred_element_type=F32, **kw)


def nt(a, b, **kw):
    return lax.dot_general(a, b, (((1,), (1,)), ((), ())), preferred_element_type=F32, **kw)


def tn(a, b, **kw):
    return lax.dot_general(a, b, (((0,), (0,)), ((), ())), preferred_element_type=F32, **kw)


def kernel(
    dims, q_ref, k_ref, v_ref, cot_ref, ld_ref, gain_ref, gq_ref, gk_ref, gv_ref,
    cc, crow, kw, vw, qw, mask, sc, of, dob, gkf, gvf, stat,
    st, xr, tz, zr, uy, yr, ez, er, ex, fin,
    xds, xd, zds, zd, yds, yd, hs, hr,
    send_sem, recv_sem, dsend, drecv, hsend, hrecv,
):
    ny, nz, nx, nhd, chunks = dims
    rows = q_ref.shape[0]
    half = rows // 2
    heads = ld_ref.shape[0]
    piece = heads // nx
    nh = piece // chunks
    zr_rows = DH // nz
    exact = dict(precision=lax.Precision.HIGHEST)

    me = lax.axis_index("ctx")
    hd = lax.axis_index("head")
    x = lax.rem(me, nx)
    z = lax.rem(lax.div(me, nx), nz)
    y = lax.div(me, nx * nz)

    def x_at(i):
        return lax.rem(x + i, nx)

    def z_at(i):
        return lax.rem(z + i, nz)

    def y_at(i):
        return lax.rem(y + i, ny)

    def x_dev(i):
        return {"ctx": me - x + x_at(i), "head": hd}

    def z_dev(i):
        return {"ctx": me + (z_at(i) - z) * nx, "head": hd}

    def y_dev(i):
        return {"ctx": me + (y_at(i) - y) * (nx * nz), "head": hd}

    def h_dev(i):
        return {"ctx": me, "head": lax.rem(hd + i, nhd)}

    partners = (
        [x_dev(i) for i in range(1, nx)] + [z_dev(i) for i in range(1, nz)]
        + [y_dev(i) for i in range(1, ny)] + [h_dev(i) for i in range(1, nhd)]
    )
    barrier = pltpu.get_barrier_semaphore()
    for device in partners:
        pl.semaphore_signal(barrier, inc=1, device_id=device, device_id_type=MESH)

    copies = []

    def push(src, dst, send, recv, device):
        copy = pltpu.make_async_remote_copy(
            src_ref=src, dst_ref=dst, send_sem=send, recv_sem=recv, device_id=device, device_id_type=MESH
        )
        copy.start()
        copies.append(copy)
        return copy

    def columns(h):
        if isinstance(h, int):
            return pl.ds(h * DH, DH)
        return pl.ds(pl.multiple_of(h * DH, DH), DH)

    def order(count):
        return sorted(range(1, count), key=lambda i: -min(i, count - i))

    ld = ld_ref[...]
    r_i = lax.broadcasted_iota(jnp.int32, (rows, rows), 0)
    c_i = lax.broadcasted_iota(jnp.int32, (rows, rows), 1)
    crow[...] = nn(ld, (r_i <= c_i).astype(F32), **exact)
    cum_t = nt((r_i >= c_i).astype(F32), ld, **exact)
    end_t = cum_t[rows - 1:rows, :]
    bg_t = jnp.exp(end_t - cum_t)
    fall_t = jnp.exp(end_t)
    for h in range(heads):
        cc[h] = jnp.broadcast_to(cum_t[:, h:h + 1], (rows, DH))
        xds[h // piece, h % piece] = jnp.broadcast_to(fall_t[:, h:h + 1], (8, DH))

    pl.semaphore_wait(barrier, len(partners))

    xd_copies = [
        push(xds.at[x_at(i)], xd.at[x], dsend.at[0, i - 1], drecv.at[0, i - 1], x_dev(i)) for i in order(nx)
    ]
    xd[x] = xds[x]

    pending = {}

    def x_send(way, c):
        for i in order(nx):
            pending[way, X_OUT, c, i] = push(
                st.at[way, c, x_at(i)], xr.at[way, c, x],
                send_sem.at[way, X_OUT, c, i - 1], recv_sem.at[way, X_OUT, c, i - 1], x_dev(i),
            )
        xr[way, c, x] = st[way, c, x]

    def arrive(way, level, c, count):
        for i in order(count):
            pending[way, level, c, i].wait_recv()

    def along(way, count):
        return range(count) if way == 0 else range(count - 1, -1, -1)

    def head_of(c, p, n):
        return p * piece + c * nh + n

    for c in range(chunks):
        for p in range(nx):
            for n in range(nh):
                h = head_of(c, p, n)
                back = jnp.broadcast_to(bg_t[:, h:h + 1], (rows, DH))
                weighted = (k_ref[:, columns(h)].astype(F32) * back).astype(BF16)
                kw[:, columns(h)] = weighted
                st[0, c, p, n] = tn(weighted, v_ref[:, columns(h)])
        x_send(0, c)

    def z_decays():
        for copy in xd_copies:
            copy.wait_recv()
        total = xd[0]
        for s in range(1, nx):
            total = total * xd[s]
        zds[...] = total
        zd[z] = total
        return [push(zds, zd.at[z], dsend.at[1, i - 1], drecv.at[1, i - 1], z_dev(i)) for i in order(nz)]

    def y_decays(zd_copies):
        for copy in zd_copies:
            copy.wait_recv()
        total = zd[0]
        for s in range(1, nz):
            total = total * zd[s]
        yds[...] = total
        yd[y] = total
        return [push(yds, yd.at[y], dsend.at[2, i - 1], drecv.at[2, i - 1], y_dev(i)) for i in order(ny)]

    def x_reduce(way, c):
        arrive(way, X_OUT, c, nx)
        for n in range(nh):
            path = list(along(way, nx))
            total = xr[way, c, path[0], n]
            for s in path[1:]:
                total = xd[s, c * nh + n, 0:1, :] * total + xr[way, c, s, n]
            tz[way, c, n] = total
        for i in order(nz):
            pending[way, Z_OUT, c, i] = push(
                tz.at[way, c, :, pl.ds(z_at(i) * zr_rows, zr_rows), :], zr.at[way, c, z],
                send_sem.at[way, Z_OUT, c, i - 1], recv_sem.at[way, Z_OUT, c, i - 1], z_dev(i),
            )
        zr[way, c, z] = tz[way, c, :, pl.ds(z * zr_rows, zr_rows), :]

    def z_reduce(way, c):
        arrive(way, Z_OUT, c, nz)
        for n in range(nh):
            path = list(along(way, nz))
            total = zr[way, c, path[0], n]
            for s in path[1:]:
                total = zd[s, c * nh + n, 0:1, :] * total + zr[way, c, s, n]
            uy[way, c, n] = total
        for i in order(ny):
            pending[way, Y_ALL, c, i] = push(
                uy.at[way, c], yr.at[way, c, y],
                send_sem.at[way, Y_ALL, c, i - 1], recv_sem.at[way, Y_ALL, c, i - 1], y_dev(i),
            )
        yr[way, c, y] = uy[way, c]

    def z_expand(way, c):
        arrive(way, Y_ALL, c, ny)
        for n in range(nh):
            state = jnp.zeros((zr_rows, DH), F32)
            for s in along(way, ny):
                longer = yd[s, c * nh + n, 0:1, :] * state + yr[way, c, s, n]
                before = (s < y) if way == 0 else (s > y)
                state = jnp.where(before, longer, state)
            for s in along(way, nz):
                ez[way, c, s, n] = state
                state = zd[s, c * nh + n, 0:1, :] * state + zr[way, c, s, n]
        for i in order(nz):
            pending[way, Z_BACK, c, i] = push(
                ez.at[way, c, z_at(i)], er.at[way, c, :, pl.ds(z * zr_rows, zr_rows), :],
                send_sem.at[way, Z_BACK, c, i - 1], recv_sem.at[way, Z_BACK, c, i - 1], z_dev(i),
            )
        er[way, c, :, pl.ds(z * zr_rows, zr_rows), :] = ez[way, c, z]

    def x_expand(way, c):
        arrive(way, Z_BACK, c, nz)
        for n in range(nh):
            state = er[way, c, n]
            for s in along(way, nx):
                ex[way, c, s, n] = state
                state = xd[s, c * nh + n, 0:1, :] * state + xr[way, c, s, n]
        for i in order(nx):
            pending[way, X_BACK, c, i] = push(
                ex.at[way, c, x_at(i)], fin.at[way, c, x],
                send_sem.at[way, X_BACK, c, i - 1], recv_sem.at[way, X_BACK, c, i - 1], x_dev(i),
            )
        fin[way, c, x] = ex[way, c, x]

    def loop(count, body):
        pair = 2 if count % 2 == 0 else 1

        def step(j, carry):
            for u in range(pair):
                body(j * pair + u)
            return carry

        lax.fori_loop(0, count // pair, step, 0)

    lower = (
        lax.broadcasted_iota(jnp.int32, (half, half), 0) >= lax.broadcasted_iota(jnp.int32, (half, half), 1)
    )

    def forward_work(h):
        here = columns(h)
        col = cc[h]
        line = crow[pl.ds(h, 1), :]
        m00 = jnp.where(lower, jnp.exp(jnp.minimum(col[:half] - line[:, :half], 0.0)), 0.0)
        m10 = jnp.exp(jnp.minimum(col[half:] - line[:, :half], 0.0))
        m11 = jnp.where(lower, jnp.exp(jnp.minimum(col[half:] - line[:, half:], 0.0)), 0.0)
        mask[h, 0], mask[h, 1], mask[h, 2] = m00, m10, m11
        q, k, v = q_ref[:, here], k_ref[:, here], v_ref[:, here]
        top = (nt(q[:half], k[:half]) * m00).astype(BF16)
        bottom = nt(q[half:], k)
        low_left = (bottom[:, :half] * m10).astype(BF16)
        low_right = (bottom[:, half:] * m11).astype(BF16)
        sc[h, 0], sc[h, 1], sc[h, 2] = top, low_left, low_right
        of[:half, here] = nn(top, v[:half])
        of[half:, here] = nn(low_left, v[:half]) + nn(low_right, v[half:])
        qw[:, here] = (q.astype(F32) * jnp.exp(col)).astype(BF16)
        vw[:, here] = (v.astype(F32) * jnp.exp(col[rows - 1:rows, :] - col)).astype(BF16)

    def enter(c):
        arrive(0, X_BACK, c, nx)

        def one(j):
            p, n = lax.div(j, nh), lax.rem(j, nh)
            here = columns(head_of(c, p, n))
            out = of[:, here] + nn(qw[:, here], fin[0, c, p, n].astype(BF16))
            of[:, here] = out
            scaled = gain_ref[:, here] * cot_ref[:, here].astype(F32)
            stat[0] += out * out
            stat[1] += out * scaled

        loop(nx * nh, one)

    def backward_work(c):
        def one(j):
            p, n = lax.div(j, nh), lax.rem(j, nh)
            h = head_of(c, p, n)
            here = columns(h)
            d_out = dob[:, here]
            q, k, v = q_ref[:, here], k_ref[:, here], v_ref[:, here]
            top = (nt(d_out[:half], v[:half]) * mask[h, 0]).astype(BF16)
            bottom = nt(d_out[half:], v)
            low_left = (bottom[:, :half] * mask[h, 1]).astype(BF16)
            low_right = (bottom[:, half:] * mask[h, 2]).astype(BF16)
            entry = fin[0, c, p, n].astype(BF16)
            weighted = (d_out.astype(F32) * jnp.exp(cc[h])).astype(BF16)
            cross = nt(weighted, entry)
            gq_ref[:half, here] = (nn(top, k[:half]) + cross[:half]).astype(BF16)
            gq_ref[half:, here] = (nn(low_left, k[:half]) + nn(low_right, k[half:]) + cross[half:]).astype(BF16)
            gkf[:half, here] = tn(top, q[:half]) + tn(low_left, q[half:])
            gkf[half:, here] = tn(low_right, q[half:])
            gvf[:half, here] = tn(sc[h, 0], d_out[:half]) + tn(sc[h, 1], d_out[half:])
            gvf[half:, here] = tn(sc[h, 2], d_out[half:])

        loop(nx * nh, one)

    def leave(c):
        arrive(1, X_BACK, c, nx)

        def one(j):
            p, n = lax.div(j, nh), lax.rem(j, nh)
            here = columns(head_of(c, p, n))
            low = fin[1, c, p, n].astype(BF16)
            gk_ref[:, here] = (gkf[:, here] + nt(vw[:, here], low)).astype(BF16)
            gv_ref[:, here] = (gvf[:, here] + nn(kw[:, here], low)).astype(BF16)

        loop(nx * nh, one)

    def scan(way, tasks, last):
        tasks = iter(tasks)
        levels = [x_reduce, z_reduce, z_expand, x_expand]

        def fill(count):
            for task in itertools.islice(tasks, count):
                task()

        for step in range(chunks + len(levels)):
            for lag in range(len(levels), -1, -1):
                c = step - lag
                if 0 <= c < chunks:
                    if lag == len(levels):
                        fill(None)
                        last(c)
                    else:
                        levels[lag](way, c)
            fill(1)
        fill(None)

    group = max(heads // chunks, 1)

    def forward_group(g):
        loop(group, lambda j: forward_work(g * group + j))

    stat[...] = jnp.zeros_like(stat)
    zd_copies = z_decays()
    forward_group(0)
    yd_copies = y_decays(zd_copies)
    if chunks > 1:
        forward_group(1)
    for copy in yd_copies:
        copy.wait_recv()
    scan(0, [functools.partial(forward_group, g) for g in range(2, chunks)], enter)

    ones = jnp.ones((8, DH), F32)
    pick = lax.broadcasted_iota(jnp.int32, (8, rows), 0) < 4
    hs[...] = jnp.where(pick, nt(ones, stat[0], **exact), nt(ones, stat[1], **exact))
    hr[hd] = hs[...]
    h_copies = [push(hs, hr.at[hd], hsend.at[i - 1], hrecv.at[i - 1], h_dev(i)) for i in order(nhd)]
    for copy in h_copies:
        copy.wait_recv()
    both = hr[0]
    for s in range(1, nhd):
        both = both + hr[s]
    features = nhd * q_ref.shape[1]
    where = lax.broadcasted_iota(jnp.int32, (8, DH), 0)
    square_sum = tn(both, (where == 0).astype(F32), **exact)
    inner_sum = tn(both, (where == 4).astype(F32), **exact)
    root_mean = jnp.sqrt(square_sum / features + eps_norm)
    stat[0] = 1.0 / root_mean
    stat[1] = inner_sum / (features * root_mean * root_mean * root_mean)

    for c in range(chunks):
        def one(j, c=c):
            p, n = lax.div(j, nh), lax.rem(j, nh)
            here = columns(head_of(c, p, n))
            scaled = gain_ref[:, here] * cot_ref[:, here].astype(F32)
            d_out = (scaled * stat[0] - of[:, here] * stat[1]).astype(BF16)
            dob[:, here] = d_out
            st[1, c, p, n] = tn(qw[:, here], d_out)

        loop(nx * nh, one)
        x_send(1, c)

    backward_work(0)
    scan(1, [functools.partial(backward_work, c) for c in range(1, chunks)], leave)

    for copy in copies:
        copy.wait_send()


def shards(dims, queries, key_rows, value_rows, cotangent, log_decay, norm_gain):
    ny, nz, nx, nhd, chunks = dims
    rows, width = queries.shape
    heads = log_decay.shape[0]
    piece = heads // nx
    nh = piece // chunks
    zrows = DH // nz
    half = rows // 2
    vmem = pltpu.VMEM
    dma = pltpu.SemaphoreType.DMA
    most = max(nx, ny, nz) - 1
    scratch = [
        vmem((heads, rows, DH), F32),
        vmem((heads, rows), F32),
        vmem((rows, width), BF16),
        vmem((rows, width), BF16),
        vmem((rows, width), BF16),
        vmem((heads, 3, half, half), F32),
        vmem((heads, 3, half, half), BF16),
        vmem((rows, width), F32),
        vmem((rows, width), BF16),
        vmem((rows, width), F32),
        vmem((rows, width), F32),
        vmem((2, rows, DH), F32),
        vmem((2, chunks, nx, nh, DH, DH), F32),
        vmem((2, chunks, nx, nh, DH, DH), F32),
        vmem((2, chunks, nh, DH, DH), F32),
        vmem((2, chunks, nz, nh, zrows, DH), F32),
        vmem((2, chunks, nh, zrows, DH), F32),
        vmem((2, chunks, ny, nh, zrows, DH), F32),
        vmem((2, chunks, nz, nh, zrows, DH), F32),
        vmem((2, chunks, nh, DH, DH), F32),
        vmem((2, chunks, nx, nh, DH, DH), F32),
        vmem((2, chunks, nx, nh, DH, DH), F32),
        vmem((nx, piece, 8, DH), F32),
        vmem((nx, piece, 8, DH), F32),
        vmem((piece, 8, DH), F32),
        vmem((nz, piece, 8, DH), F32),
        vmem((piece, 8, DH), F32),
        vmem((ny, piece, 8, DH), F32),
        vmem((8, rows), F32),
        vmem((nhd, 8, rows), F32),
        dma((2, 5, chunks, most)),
        dma((2, 5, chunks, most)),
        dma((3, most)),
        dma((3, most)),
        dma((max(nhd - 1, 1),)),
        dma((max(nhd - 1, 1),)),
    ]
    return pl.pallas_call(
        functools.partial(kernel, dims),
        out_shape=[jax.ShapeDtypeStruct((rows, width), BF16)] * 3,
        in_specs=[pl.BlockSpec(memory_space=pltpu.VMEM)] * 6,
        out_specs=[pl.BlockSpec(memory_space=pltpu.VMEM)] * 3,
        scratch_shapes=scratch,
        compiler_params=pltpu.CompilerParams(
            collective_id=0, has_side_effects=True, vmem_limit_bytes=56 * 1024 * 1024
        ),
    )(queries, key_rows, value_rows, cotangent, log_decay, norm_gain.reshape(1, width))


def solution(mesh):
    ny, nz, nx = PARTS[mesh.shape["ctx"]]
    dims = (ny, nz, nx, mesh.shape["head"], 4 if mesh.shape["ctx"] == 64 else 2)
    in_specs = (
        P("ctx", "head"),
        P("ctx", "head"),
        P("ctx", "head"),
        P("ctx", "head"),
        P("head", "ctx"),
        P("head"),
    )
    out_specs = (P("ctx", "head"), P("ctx", "head"), P("ctx", "head"))
    return jax.shard_map(
        functools.partial(shards, dims), mesh=mesh, in_specs=in_specs, out_specs=out_specs, check_vma=False
    )
```

```python
import functools
import itertools

import jax
import jax.numpy as jnp
from jax import lax
from jax.experimental import pallas as pl
from jax.experimental.pallas import tpu as pltpu
from jax.sharding import PartitionSpec as P

eps_norm = 1e-06
MESH = pl.DeviceIdType.MESH
F32, BF16 = jnp.float32, jnp.bfloat16
DH = 128
PARTS = {64: (4, 4, 4), 8: (2, 2, 2)}
X_OUT, Z_OUT, Y_ALL, Z_BACK, X_BACK = range(5)


def nn(a, b, **kw):
    return lax.dot_general(a, b, (((1,), (0,)), ((), ())), preferred_element_type=F32, **kw)


def nt(a, b, **kw):
    return lax.dot_general(a, b, (((1,), (1,)), ((), ())), preferred_element_type=F32, **kw)


def tn(a, b, **kw):
    return lax.dot_general(a, b, (((0,), (0,)), ((), ())), preferred_element_type=F32, **kw)


LATENCY = {"x": 3.8, "z": 4.2, "y": 3.9}
CARRY = {"x": 10.5, "z": 5.2, "y": 1.3}
FORWARD_US, BACKWARD_US = 0.4, 0.6


def timetable(chunks):
    free = {}
    events = []
    ready = [0.0] * chunks
    for level, axis in enumerate(["x", "z", "y", "z", "x"]):
        link = axis if level else "x"
        for c in range(chunks):
            begin = max(free.get(link, 0.0), ready[c])
            free[link] = begin + CARRY[axis] / chunks
            ready[c] = free[link] + LATENCY[axis]
            events.append((ready[c], level, c))
    return sorted(events)


def kernel(
    dims, q_in, k_in, v_in, cot_in, ld_in, gain_in, gq_out, gk_out, gv_out,
    q_ref, k_ref, v_ref, cot_ref, ld_ref, gain_ref, gq_ref, gk_ref, gv_ref, cc, crow, kw, vw, qw, mask, sc, of, dob, gkf, gvf, stat,
    st, xr, tz, zr, uy, yr, ez, er, ex, fin,
    xds, xd, zds, zd, yds, yd, hs, hr,
    send_sem, recv_sem, dsend, drecv, hsend, hrecv, in_sem, out_sem,
):
    ny, nz, nx, nhd, chunks = dims
    rows = q_ref.shape[0]
    half = rows // 2
    heads = ld_ref.shape[0]
    piece = heads // nx
    nh = piece // chunks
    zr_rows = DH // nz
    exact = dict(precision=lax.Precision.HIGHEST)

    me = lax.axis_index("ctx")
    hd = lax.axis_index("head")
    x = lax.rem(me, nx)
    z = lax.rem(lax.div(me, nx), nz)
    y = lax.div(me, nx * nz)

    def x_at(i):
        return lax.rem(x + i, nx)

    def z_at(i):
        return lax.rem(z + i, nz)

    def y_at(i):
        return lax.rem(y + i, ny)

    def x_dev(i):
        return {"ctx": me - x + x_at(i), "head": hd}

    def z_dev(i):
        return {"ctx": me + (z_at(i) - z) * nx, "head": hd}

    def y_dev(i):
        return {"ctx": me + (y_at(i) - y) * (nx * nz), "head": hd}

    def h_dev(i):
        return {"ctx": me, "head": lax.rem(hd + i, nhd)}

    partners = (
        [x_dev(i) for i in range(1, nx)] + [z_dev(i) for i in range(1, nz)]
        + [y_dev(i) for i in range(1, ny)] + [h_dev(i) for i in range(1, nhd)]
    )
    barrier = pltpu.get_barrier_semaphore()
    for device in partners:
        pl.semaphore_signal(barrier, inc=1, device_id=device, device_id_type=MESH)

    def load(i, src, dst):
        copy = pltpu.make_async_copy(src, dst, in_sem.at[i])
        copy.start()
        return copy

    ld_load = load(0, ld_in, ld_ref)
    k_load = load(1, k_in, k_ref)
    v_load = load(2, v_in, v_ref)
    q_load = load(3, q_in, q_ref)
    cot_load = load(4, cot_in, cot_ref)
    gain_load = load(5, gain_in, gain_ref)

    copies = []

    def push(src, dst, send, recv, device):
        copy = pltpu.make_async_remote_copy(
            src_ref=src, dst_ref=dst, send_sem=send, recv_sem=recv, device_id=device, device_id_type=MESH
        )
        copy.start()
        copies.append(copy)
        return copy

    def columns(h):
        if isinstance(h, int):
            return pl.ds(h * DH, DH)
        return pl.ds(pl.multiple_of(h * DH, DH), DH)

    def order(count):
        return sorted(range(1, count), key=lambda i: -min(i, count - i))

    ld_load.wait()
    ld = ld_ref[...]
    r_i = lax.broadcasted_iota(jnp.int32, (rows, rows), 0)
    c_i = lax.broadcasted_iota(jnp.int32, (rows, rows), 1)
    crow[...] = nn(ld, (r_i <= c_i).astype(F32), **exact)
    cum_t = nt((r_i >= c_i).astype(F32), ld, **exact)
    end_t = cum_t[rows - 1:rows, :]
    bg_t = jnp.exp(end_t - cum_t)
    fall_t = jnp.exp(end_t)
    for h in range(heads):
        cc[h] = jnp.broadcast_to(cum_t[:, h:h + 1], (rows, DH))
        xds[h // piece, h % piece] = jnp.broadcast_to(fall_t[:, h:h + 1], (8, DH))

    xd[x] = xds[x]

    pending = {}

    def x_send(way, c):
        for i in order(nx):
            pending[way, X_OUT, c, i] = push(
                st.at[way, c, x_at(i)], xr.at[way, c, x],
                send_sem.at[way, X_OUT, c, i - 1], recv_sem.at[way, X_OUT, c, i - 1], x_dev(i),
            )
        xr[way, c, x] = st[way, c, x]

    def arrive(way, level, c, count):
        for i in order(count):
            pending[way, level, c, i].wait_recv()

    def along(way, count):
        return range(count) if way == 0 else range(count - 1, -1, -1)

    def head_of(c, p, n):
        return p * piece + c * nh + n

    k_load.wait()
    v_load.wait()
    decay_copies = {}
    for c in range(chunks):
        for p in range(nx):
            for n in range(nh):
                h = head_of(c, p, n)
                back = jnp.broadcast_to(bg_t[:, h:h + 1], (rows, DH))
                weighted = (k_ref[:, columns(h)].astype(F32) * back).astype(BF16)
                kw[:, columns(h)] = weighted
                st[0, c, p, n] = tn(weighted, v_ref[:, columns(h)])
        if c == 0:
            pl.semaphore_wait(barrier, len(partners))
            decay_copies[X_OUT] = [
                push(xds.at[x_at(i)], xd.at[x], dsend.at[0, i - 1], drecv.at[0, i - 1], x_dev(i)) for i in order(nx)
            ]
        x_send(0, c)

    def z_decays():
        for copy in decay_copies[X_OUT]:
            copy.wait_recv()
        total = xd[0]
        for s in range(1, nx):
            total = total * xd[s]
        zds[...] = total
        zd[z] = total
        decay_copies[Z_OUT] = [
            push(zds, zd.at[z], dsend.at[1, i - 1], drecv.at[1, i - 1], z_dev(i)) for i in order(nz)
        ]

    def y_decays():
        for copy in decay_copies[Z_OUT]:
            copy.wait_recv()
        total = zd[0]
        for s in range(1, nz):
            total = total * zd[s]
        yds[...] = total
        yd[y] = total
        decay_copies[Y_ALL] = [
            push(yds, yd.at[y], dsend.at[2, i - 1], drecv.at[2, i - 1], y_dev(i)) for i in order(ny)
        ]

    def x_reduce(way, c):
        arrive(way, X_OUT, c, nx)
        if way == 0 and c == 0:
            z_decays()
        for n in range(nh):
            path = list(along(way, nx))
            total = xr[way, c, path[0], n]
            for s in path[1:]:
                total = xd[s, c * nh + n, 0:1, :] * total + xr[way, c, s, n]
            tz[way, c, n] = total
        for i in order(nz):
            pending[way, Z_OUT, c, i] = push(
                tz.at[way, c, :, pl.ds(z_at(i) * zr_rows, zr_rows), :], zr.at[way, c, z],
                send_sem.at[way, Z_OUT, c, i - 1], recv_sem.at[way, Z_OUT, c, i - 1], z_dev(i),
            )
        zr[way, c, z] = tz[way, c, :, pl.ds(z * zr_rows, zr_rows), :]

    def z_reduce(way, c):
        arrive(way, Z_OUT, c, nz)
        if way == 0 and c == 0:
            y_decays()
        for n in range(nh):
            path = list(along(way, nz))
            total = zr[way, c, path[0], n]
            for s in path[1:]:
                total = zd[s, c * nh + n, 0:1, :] * total + zr[way, c, s, n]
            uy[way, c, n] = total
        for i in order(ny):
            pending[way, Y_ALL, c, i] = push(
                uy.at[way, c], yr.at[way, c, y],
                send_sem.at[way, Y_ALL, c, i - 1], recv_sem.at[way, Y_ALL, c, i - 1], y_dev(i),
            )
        yr[way, c, y] = uy[way, c]

    def z_expand(way, c):
        arrive(way, Y_ALL, c, ny)
        if way == 0 and c == 0:
            for copy in decay_copies[Y_ALL]:
                copy.wait_recv()
        for n in range(nh):
            state = jnp.zeros((zr_rows, DH), F32)
            for s in along(way, ny):
                longer = yd[s, c * nh + n, 0:1, :] * state + yr[way, c, s, n]
                before = (s < y) if way == 0 else (s > y)
                state = jnp.where(before, longer, state)
            for s in along(way, nz):
                ez[way, c, s, n] = state
                state = zd[s, c * nh + n, 0:1, :] * state + zr[way, c, s, n]
        for i in order(nz):
            pending[way, Z_BACK, c, i] = push(
                ez.at[way, c, z_at(i)], er.at[way, c, :, pl.ds(z * zr_rows, zr_rows), :],
                send_sem.at[way, Z_BACK, c, i - 1], recv_sem.at[way, Z_BACK, c, i - 1], z_dev(i),
            )
        er[way, c, :, pl.ds(z * zr_rows, zr_rows), :] = ez[way, c, z]

    def x_expand(way, c):
        arrive(way, Z_BACK, c, nz)
        for n in range(nh):
            state = er[way, c, n]
            for s in along(way, nx):
                ex[way, c, s, n] = state
                state = xd[s, c * nh + n, 0:1, :] * state + xr[way, c, s, n]
        for i in order(nx):
            pending[way, X_BACK, c, i] = push(
                ex.at[way, c, x_at(i)], fin.at[way, c, x],
                send_sem.at[way, X_BACK, c, i - 1], recv_sem.at[way, X_BACK, c, i - 1], x_dev(i),
            )
        fin[way, c, x] = ex[way, c, x]

    def loop(count, body):
        pair = 2 if count % 2 == 0 else 1

        def step(j, carry):
            for u in range(pair):
                body(j * pair + u)
            return carry

        lax.fori_loop(0, count // pair, step, 0)

    lower = (
        lax.broadcasted_iota(jnp.int32, (half, half), 0) >= lax.broadcasted_iota(jnp.int32, (half, half), 1)
    )

    def forward_work(h):
        here = columns(h)
        col = cc[h]
        line = crow[pl.ds(h, 1), :]
        m00 = jnp.where(lower, jnp.exp(jnp.minimum(col[:half] - line[:, :half], 0.0)), 0.0)
        m10 = jnp.exp(jnp.minimum(col[half:] - line[:, :half], 0.0))
        m11 = jnp.where(lower, jnp.exp(jnp.minimum(col[half:] - line[:, half:], 0.0)), 0.0)
        mask[h, 0], mask[h, 1], mask[h, 2] = m00, m10, m11
        q, k, v = q_ref[:, here], k_ref[:, here], v_ref[:, here]
        top = (nt(q[:half], k[:half]) * m00).astype(BF16)
        bottom = nt(q[half:], k)
        low_left = (bottom[:, :half] * m10).astype(BF16)
        low_right = (bottom[:, half:] * m11).astype(BF16)
        sc[h, 0], sc[h, 1], sc[h, 2] = top, low_left, low_right
        of[:half, here] = nn(top, v[:half])
        of[half:, here] = nn(low_left, v[:half]) + nn(low_right, v[half:])
        qw[:, here] = (q.astype(F32) * jnp.exp(col)).astype(BF16)
        vw[:, here] = (v.astype(F32) * jnp.exp(col[rows - 1:rows, :] - col)).astype(BF16)

    def enter(c):
        arrive(0, X_BACK, c, nx)

        def one(j):
            p, n = lax.div(j, nh), lax.rem(j, nh)
            here = columns(head_of(c, p, n))
            out = of[:, here] + nn(qw[:, here], fin[0, c, p, n].astype(BF16))
            of[:, here] = out
            scaled = gain_ref[:, here] * cot_ref[:, here].astype(F32)
            stat[0] += out * out
            stat[1] += out * scaled

        loop(nx * nh, one)

    def backward_work(c):
        def one(j):
            p, n = lax.div(j, nh), lax.rem(j, nh)
            h = head_of(c, p, n)
            here = columns(h)
            d_out = dob[:, here]
            q, k, v = q_ref[:, here], k_ref[:, here], v_ref[:, here]
            top = (nt(d_out[:half], v[:half]) * mask[h, 0]).astype(BF16)
            bottom = nt(d_out[half:], v)
            low_left = (bottom[:, :half] * mask[h, 1]).astype(BF16)
            low_right = (bottom[:, half:] * mask[h, 2]).astype(BF16)
            entry = fin[0, c, p, n].astype(BF16)
            weighted = (d_out.astype(F32) * jnp.exp(cc[h])).astype(BF16)
            cross = nt(weighted, entry)
            gq_ref[:half, here] = (nn(top, k[:half]) + cross[:half]).astype(BF16)
            gq_ref[half:, here] = (nn(low_left, k[:half]) + nn(low_right, k[half:]) + cross[half:]).astype(BF16)
            gkf[:half, here] = tn(top, q[:half]) + tn(low_left, q[half:])
            gkf[half:, here] = tn(low_right, q[half:])
            gvf[:half, here] = tn(sc[h, 0], d_out[:half]) + tn(sc[h, 1], d_out[half:])
            gvf[half:, here] = tn(sc[h, 2], d_out[half:])

        loop(nx * nh, one)

    def leave(c):
        arrive(1, X_BACK, c, nx)

        def one(j):
            p, n = lax.div(j, nh), lax.rem(j, nh)
            here = columns(head_of(c, p, n))
            low = fin[1, c, p, n].astype(BF16)
            gk_ref[:, here] = (gkf[:, here] + nt(vw[:, here], low)).astype(BF16)
            gv_ref[:, here] = (gvf[:, here] + nn(kw[:, here], low)).astype(BF16)

        loop(nx * nh, one)

    def scan(way, tasks, work, last):
        levels = [x_reduce, z_reduce, z_expand, x_expand, lambda way, c: last(c)]
        tasks = list(tasks)
        now = 0.0
        for when, level, c in timetable(chunks):
            while tasks and now + work <= when + 0.5:
                tasks.pop(0)()
                now += work
            if level == len(levels) - 1:
                while tasks:
                    tasks.pop(0)()
            levels[level](way, c)
            now = max(now, when) + 0.2

    group = max(heads // (2 * chunks), 1)

    def forward_group(g):
        loop(group, lambda j: forward_work(g * group + j))

    stat[...] = jnp.zeros_like(stat)
    q_load.wait()
    cot_load.wait()
    gain_load.wait()
    scan(0, [functools.partial(forward_group, g) for g in range(heads // group)], FORWARD_US * group, enter)

    ones = jnp.ones((8, DH), F32)
    pick = lax.broadcasted_iota(jnp.int32, (8, rows), 0) < 4
    hs[...] = jnp.where(pick, nt(ones, stat[0], **exact), nt(ones, stat[1], **exact))
    hr[hd] = hs[...]
    h_copies = [push(hs, hr.at[hd], hsend.at[i - 1], hrecv.at[i - 1], h_dev(i)) for i in order(nhd)]
    for copy in h_copies:
        copy.wait_recv()
    both = hr[0]
    for s in range(1, nhd):
        both = both + hr[s]
    features = nhd * q_ref.shape[1]
    where = lax.broadcasted_iota(jnp.int32, (8, DH), 0)
    square_sum = tn(both, (where == 0).astype(F32), **exact)
    inner_sum = tn(both, (where == 4).astype(F32), **exact)
    root_mean = jnp.sqrt(square_sum / features + eps_norm)
    stat[0] = 1.0 / root_mean
    stat[1] = inner_sum / (features * root_mean * root_mean * root_mean)

    for c in range(chunks):
        def one(j, c=c):
            p, n = lax.div(j, nh), lax.rem(j, nh)
            here = columns(head_of(c, p, n))
            scaled = gain_ref[:, here] * cot_ref[:, here].astype(F32)
            d_out = (scaled * stat[0] - of[:, here] * stat[1]).astype(BF16)
            dob[:, here] = d_out
            st[1, c, p, n] = tn(qw[:, here], d_out)

        loop(nx * nh, one)
        x_send(1, c)

    def flush(i, src, dst):
        copy = pltpu.make_async_copy(src, dst, out_sem.at[i])
        copy.start()
        return copy

    stores = []

    def end(c):
        if c == 0:
            stores.append(flush(0, gq_ref, gq_out))
        leave(c)
        for p in range(nx):
            for n in range(nh):
                h = head_of(c, p, n)
                stores.append(flush(1 + 2 * h, gk_ref.at[:, columns(h)], gk_out.at[:, columns(h)]))
                stores.append(flush(2 + 2 * h, gv_ref.at[:, columns(h)], gv_out.at[:, columns(h)]))

    scan(1, [functools.partial(backward_work, c) for c in range(chunks)], BACKWARD_US * nx * nh, end)
    for copy in stores:
        copy.wait()

    for copy in copies:
        copy.wait_send()


SLICES = 4


def hand_over(a_in, b_in, c_in, a_out, b_out, c_out, held, in_sem, out_sem):
    reads, writes = [], []
    for i, (src, dst) in enumerate([(a_in, a_out), (b_in, b_out), (c_in, c_out)]):
        rows = src.shape[0] // SLICES
        for j in range(SLICES):
            part = pl.ds(j * rows, rows)
            reads.append(pltpu.make_async_copy(src.at[part], held.at[i, part], in_sem.at[i, j]))
            writes.append(pltpu.make_async_copy(held.at[i, part], dst.at[part], out_sem.at[i, j]))
    for read in reads:
        read.start()
    for read, write in zip(reads, writes):
        read.wait()
        write.start()
    for write in writes:
        write.wait()


def shards(dims, queries, key_rows, value_rows, cotangent, log_decay, norm_gain):
    ny, nz, nx, nhd, chunks = dims
    rows, width = queries.shape
    heads = log_decay.shape[0]
    piece = heads // nx
    nh = piece // chunks
    zrows = DH // nz
    half = rows // 2
    vmem = pltpu.VMEM
    dma = pltpu.SemaphoreType.DMA
    most = max(nx, ny, nz) - 1
    scratch = [
        vmem((rows, width), BF16),
        vmem((rows, width), BF16),
        vmem((rows, width), BF16),
        vmem((rows, width), BF16),
        vmem((heads, rows), F32),
        vmem((1, width), F32),
        vmem((rows, width), BF16),
        vmem((rows, width), BF16),
        vmem((rows, width), BF16),
        vmem((heads, rows, DH), F32),
        vmem((heads, rows), F32),
        vmem((rows, width), BF16),
        vmem((rows, width), BF16),
        vmem((rows, width), BF16),
        vmem((heads, 3, half, half), F32),
        vmem((heads, 3, half, half), BF16),
        vmem((rows, width), F32),
        vmem((rows, width), BF16),
        vmem((rows, width), F32),
        vmem((rows, width), F32),
        vmem((2, rows, DH), F32),
        vmem((2, chunks, nx, nh, DH, DH), F32),
        vmem((2, chunks, nx, nh, DH, DH), F32),
        vmem((2, chunks, nh, DH, DH), F32),
        vmem((2, chunks, nz, nh, zrows, DH), F32),
        vmem((2, chunks, nh, zrows, DH), F32),
        vmem((2, chunks, ny, nh, zrows, DH), F32),
        vmem((2, chunks, nz, nh, zrows, DH), F32),
        vmem((2, chunks, nh, DH, DH), F32),
        vmem((2, chunks, nx, nh, DH, DH), F32),
        vmem((2, chunks, nx, nh, DH, DH), F32),
        vmem((nx, piece, 8, DH), F32),
        vmem((nx, piece, 8, DH), F32),
        vmem((piece, 8, DH), F32),
        vmem((nz, piece, 8, DH), F32),
        vmem((piece, 8, DH), F32),
        vmem((ny, piece, 8, DH), F32),
        vmem((8, rows), F32),
        vmem((nhd, 8, rows), F32),
        dma((2, 5, chunks, most)),
        dma((2, 5, chunks, most)),
        dma((3, most)),
        dma((3, most)),
        dma((max(nhd - 1, 1),)),
        dma((max(nhd - 1, 1),)),
        dma((6,)),
        dma((1 + 2 * heads,)),
    ]
    grads = pl.pallas_call(
        functools.partial(kernel, dims),
        out_shape=[jax.ShapeDtypeStruct((rows, width), BF16)] * 3,
        in_specs=[pl.BlockSpec(memory_space=pl.ANY)] * 6,
        out_specs=[pl.BlockSpec(memory_space=pl.ANY)] * 3,
        scratch_shapes=scratch,
        compiler_params=pltpu.CompilerParams(
            collective_id=0, has_side_effects=True, vmem_limit_bytes=56 * 1024 * 1024
        ),
    )(queries, key_rows, value_rows, cotangent, log_decay, norm_gain.reshape(1, width))
    return pl.pallas_call(
        hand_over,
        out_shape=[jax.ShapeDtypeStruct((rows, width), BF16)] * 3,
        in_specs=[pl.BlockSpec(memory_space=pl.ANY)] * 3,
        out_specs=[pl.BlockSpec(memory_space=pl.ANY)] * 3,
        scratch_shapes=[vmem((3, rows, width), BF16), dma((3, SLICES)), dma((3, SLICES))],
        compiler_params=pltpu.CompilerParams(vmem_limit_bytes=56 * 1024 * 1024),
    )(*grads)


def solution(mesh):
    ny, nz, nx = PARTS[mesh.shape["ctx"]]
    dims = (ny, nz, nx, mesh.shape["head"], 4 if mesh.shape["ctx"] == 64 else 2)
    in_specs = (
        P("ctx", "head"),
        P("ctx", "head"),
        P("ctx", "head"),
        P("ctx", "head"),
        P("head", "ctx"),
        P("head"),
    )
    out_specs = (P("ctx", "head"), P("ctx", "head"), P("ctx", "head"))
    return jax.shard_map(
        functools.partial(shards, dims), mesh=mesh, in_specs=in_specs, out_specs=out_specs, check_vma=False
    )
```

```python
import functools

import jax
import jax.numpy as jnp
from jax import lax
from jax.experimental import pallas as pl
from jax.experimental.pallas import tpu as pltpu
from jax.sharding import PartitionSpec as P

eps_norm = 1e-06
MESH = pl.DeviceIdType.MESH
F32, BF16 = jnp.float32, jnp.bfloat16
DH = 128
PARTS = {64: (4, 4, 4), 8: (2, 2, 2)}
X_OUT, Z_OUT, Y_ALL, Z_BACK, X_BACK = range(5)


def nn(a, b, **kw):
    return lax.dot_general(a, b, (((1,), (0,)), ((), ())), preferred_element_type=F32, **kw)


def nt(a, b, **kw):
    return lax.dot_general(a, b, (((1,), (1,)), ((), ())), preferred_element_type=F32, **kw)


def tn(a, b, **kw):
    return lax.dot_general(a, b, (((0,), (0,)), ((), ())), preferred_element_type=F32, **kw)


LATENCY = {"x": 3.5, "z": 4.0, "y": 3.5}
CARRY = {"x": 10.5, "z": 5.2, "y": 1.3}
FORWARD_US, BACKWARD_US, EVENT_US, SLACK_US = 0.22, 0.38, 0.1, 0.3
CUTS = 2


def timetable(chunks):
    free = {}
    events = []
    ready = [0.0] * chunks
    for level, axis in enumerate(["x", "z", "y", "z", "x"]):
        link = axis if level else "x"
        for c in range(chunks):
            begin = max(free.get(link, 0.0), ready[c])
            free[link] = begin + CARRY[axis] / chunks
            ready[c] = free[link] + LATENCY[axis]
            events.append((ready[c], level, c))
    return sorted(events)


def kernel(
    dims, q_in, k_in, v_in, cot_in, ld_in, gain_in, gq_out, gk_out, gv_out,
    q_ref, k_ref, v_ref, cot_ref, ld_ref, gain_ref, gq_ref, gk_ref, gv_ref, cc, crow, kw, vw, qw, mask, sc, of, dob, gkf, gvf, stat,
    st, xr, tz, zr, uy, yr, ez, er, ex, fin,
    xds, xd, zds, zd, yds, yd, hs, hr,
    send_sem, recv_sem, dsend, drecv, hsend, hrecv, in_sem, out_sem,
):
    ny, nz, nx, nhd = dims
    rows = q_ref.shape[0]
    half = rows // 2
    heads = ld_ref.shape[0]
    piece = heads // nx
    chunks = piece * CUTS
    cut = DH // CUTS
    strip = cut // nz
    exact = dict(precision=lax.Precision.HIGHEST)

    me = lax.axis_index("ctx")
    hd = lax.axis_index("head")
    x = lax.rem(me, nx)
    z = lax.rem(lax.div(me, nx), nz)
    y = lax.div(me, nx * nz)

    def x_at(i):
        return lax.rem(x + i, nx)

    def z_at(i):
        return lax.rem(z + i, nz)

    def y_at(i):
        return lax.rem(y + i, ny)

    def x_dev(i):
        return {"ctx": me - x + x_at(i), "head": hd}

    def z_dev(i):
        return {"ctx": me + (z_at(i) - z) * nx, "head": hd}

    def y_dev(i):
        return {"ctx": me + (y_at(i) - y) * (nx * nz), "head": hd}

    def h_dev(i):
        return {"ctx": me, "head": lax.rem(hd + i, nhd)}

    partners = (
        [x_dev(i) for i in range(1, nx)] + [z_dev(i) for i in range(1, nz)]
        + [y_dev(i) for i in range(1, ny)] + [h_dev(i) for i in range(1, nhd)]
    )
    barrier = pltpu.get_barrier_semaphore()
    for device in partners:
        pl.semaphore_signal(barrier, inc=1, device_id=device, device_id_type=MESH)

    def load(i, src, dst):
        copy = pltpu.make_async_copy(src, dst, in_sem.at[i])
        copy.start()
        return copy

    ld_load = load(0, ld_in, ld_ref)
    k_load = load(1, k_in, k_ref)
    v_load = load(2, v_in, v_ref)
    q_load = load(3, q_in, q_ref)
    cot_load = load(4, cot_in, cot_ref)
    gain_load = load(5, gain_in, gain_ref)

    def push(src, dst, send, recv, device):
        copy = pltpu.make_async_remote_copy(
            src_ref=src, dst_ref=dst, send_sem=send, recv_sem=recv, device_id=device, device_id_type=MESH
        )
        copy.start()
        return copy

    def columns(h):
        if isinstance(h, int):
            return pl.ds(h * DH, DH)
        return pl.ds(pl.multiple_of(h * DH, DH), DH)

    def order(count):
        return sorted(range(1, count), key=lambda i: -min(i, count - i))

    ld_load.wait()
    ld = ld_ref[...]
    r_i = lax.broadcasted_iota(jnp.int32, (rows, rows), 0)
    c_i = lax.broadcasted_iota(jnp.int32, (rows, rows), 1)
    crow[...] = nn(ld, (r_i <= c_i).astype(F32), **exact)
    cum_t = nt((r_i >= c_i).astype(F32), ld, **exact)
    end_t = cum_t[rows - 1:rows, :]
    bg_t = jnp.exp(end_t - cum_t)
    fall_t = jnp.exp(end_t)
    for h in range(heads):
        cc[h] = jnp.broadcast_to(cum_t[:, h:h + 1], (rows, DH))
        xds[h // piece, h % piece] = jnp.broadcast_to(fall_t[:, h:h + 1], (8, DH))

    xd[x] = xds[x]

    def x_send(way, c):
        for i in order(nx):
            push(
                st.at[way, c, x_at(i)], xr.at[way, c, x],
                send_sem.at[way, X_OUT, c], recv_sem.at[way, X_OUT, c], x_dev(i),
            )
        xr[way, c, x] = st[way, c, x]

    def arrive(way, level, c):
        size = sizes(level, way, c)
        pltpu.make_async_copy(size, size, recv_sem.at[way, level, c]).wait()

    def leave_behind(way):
        for level in range(5):
            for c in range(chunks):
                size = sizes(level, way, c)
                pltpu.make_async_copy(size, size, send_sem.at[way, level, c]).wait()

    def sizes(level, way, c):
        if level in (X_OUT, X_BACK):
            return xr.at[way, c, pl.ds(0, nx - 1)]
        return (zr if level in (Z_OUT, Z_BACK) else yr).at[way, c, pl.ds(0, (ny if level == Y_ALL else nz) - 1)]

    def along(way, count):
        return range(count) if way == 0 else range(count - 1, -1, -1)

    def keep(way, g, p, state):
        for u in range(CUTS):
            st[way, g * CUTS + u, p] = state[u * cut:(u + 1) * cut]

    k_load.wait()
    v_load.wait()
    decay_copies = {}
    for g in range(piece):
        for p in range(nx):
            h = p * piece + g
            back = jnp.broadcast_to(bg_t[:, h:h + 1], (rows, DH))
            weighted = (k_ref[:, columns(h)].astype(F32) * back).astype(BF16)
            kw[:, columns(h)] = weighted
            keep(0, g, p, tn(weighted, v_ref[:, columns(h)]))
        if g == 0:
            pl.semaphore_wait(barrier, len(partners))
            decay_copies[X_OUT] = [
                push(xds.at[x_at(i)], xd.at[x], dsend.at[0, i - 1], drecv.at[0, i - 1], x_dev(i)) for i in order(nx)
            ]
        for u in range(CUTS):
            x_send(0, g * CUTS + u)

    def z_decays():
        for copy in decay_copies[X_OUT]:
            copy.wait_recv()
        total = xd[0]
        for s in range(1, nx):
            total = total * xd[s]
        zds[...] = total
        zd[z] = total
        decay_copies[Z_OUT] = [
            push(zds, zd.at[z], dsend.at[1, i - 1], drecv.at[1, i - 1], z_dev(i)) for i in order(nz)
        ]

    def y_decays():
        for copy in decay_copies[Z_OUT]:
            copy.wait_recv()
        total = zd[0]
        for s in range(1, nz):
            total = total * zd[s]
        yds[...] = total
        yd[y] = total
        decay_copies[Y_ALL] = [
            push(yds, yd.at[y], dsend.at[2, i - 1], drecv.at[2, i - 1], y_dev(i)) for i in order(ny)
        ]

    def x_reduce(way, c):
        g = c // CUTS
        if way == 0 and c == 0:
            z_decays()
        arrive(way, X_OUT, c)
        path = list(along(way, nx))
        total = xr[way, c, path[0]]
        for s in path[1:]:
            total = xd[s, g, 0:1, :] * total + xr[way, c, s]
        tz[way, c] = total
        for i in order(nz):
            push(
                tz.at[way, c, pl.ds(z_at(i) * strip, strip)], zr.at[way, c, z],
                send_sem.at[way, Z_OUT, c], recv_sem.at[way, Z_OUT, c], z_dev(i),
            )
        zr[way, c, z] = tz[way, c, pl.ds(z * strip, strip)]

    def z_reduce(way, c):
        g = c // CUTS
        if way == 0 and c == 0:
            y_decays()
        arrive(way, Z_OUT, c)
        path = list(along(way, nz))
        total = zr[way, c, path[0]]
        for s in path[1:]:
            total = zd[s, g, 0:1, :] * total + zr[way, c, s]
        uy[way, c] = total
        for i in order(ny):
            push(
                uy.at[way, c], yr.at[way, c, y],
                send_sem.at[way, Y_ALL, c], recv_sem.at[way, Y_ALL, c], y_dev(i),
            )
        yr[way, c, y] = total

    def z_expand(way, c):
        g = c // CUTS
        if way == 0 and c == 0:
            for copy in decay_copies[Y_ALL]:
                copy.wait_recv()
        arrive(way, Y_ALL, c)
        state = jnp.zeros((strip, DH), F32)
        for s in along(way, ny):
            longer = yd[s, g, 0:1, :] * state + yr[way, c, s]
            before = (s < y) if way == 0 else (s > y)
            state = jnp.where(before, longer, state)
        for s in along(way, nz):
            ez[way, c, s] = state
            state = zd[s, g, 0:1, :] * state + zr[way, c, s]
        for i in order(nz):
            push(
                ez.at[way, c, z_at(i)], er.at[way, c, pl.ds(z * strip, strip)],
                send_sem.at[way, Z_BACK, c], recv_sem.at[way, Z_BACK, c], z_dev(i),
            )
        er[way, c, pl.ds(z * strip, strip)] = ez[way, c, z]

    def x_expand(way, c):
        g, u = c // CUTS, c % CUTS
        arrive(way, Z_BACK, c)
        state = er[way, c]
        for s in along(way, nx):
            ex[way, c, s] = state
            state = xd[s, g, 0:1, :] * state + xr[way, c, s]
        here = pl.ds(u * cut, cut)
        for i in order(nx):
            push(
                ex.at[way, c, x_at(i)], fin.at[way, g, x, here],
                send_sem.at[way, X_BACK, c], recv_sem.at[way, X_BACK, c], x_dev(i),
            )
        fin[way, g, x, here] = ex[way, c, x]

    def arrived(way, g):
        for u in range(CUTS):
            arrive(way, X_BACK, g * CUTS + u)

    def loop(count, body):
        pair = 2 if count % 2 == 0 else 1

        def step(j, carry):
            for u in range(pair):
                body(j * pair + u)
            return carry

        lax.fori_loop(0, count // pair, step, 0)

    lower = (
        lax.broadcasted_iota(jnp.int32, (half, half), 0) >= lax.broadcasted_iota(jnp.int32, (half, half), 1)
    )

    def forward_work(h):
        here = columns(h)
        col = cc[h]
        line = crow[pl.ds(h, 1), :]
        m00 = jnp.where(lower, jnp.exp(jnp.minimum(col[:half] - line[:, :half], 0.0)), 0.0)
        m10 = jnp.exp(jnp.minimum(col[half:] - line[:, :half], 0.0))
        m11 = jnp.where(lower, jnp.exp(jnp.minimum(col[half:] - line[:, half:], 0.0)), 0.0)
        mask[h, 0], mask[h, 1], mask[h, 2] = m00, m10, m11
        q, k, v = q_ref[:, here], k_ref[:, here], v_ref[:, here]
        top = (nt(q[:half], k[:half]) * m00).astype(BF16)
        bottom = nt(q[half:], k)
        low_left = (bottom[:, :half] * m10).astype(BF16)
        low_right = (bottom[:, half:] * m11).astype(BF16)
        sc[h, 0], sc[h, 1], sc[h, 2] = top, low_left, low_right
        of[:half, here] = nn(top, v[:half])
        of[half:, here] = nn(low_left, v[:half]) + nn(low_right, v[half:])
        qw[:, here] = (q.astype(F32) * jnp.exp(col)).astype(BF16)
        vw[:, here] = (v.astype(F32) * jnp.exp(col[rows - 1:rows, :] - col)).astype(BF16)

    def enter(g):
        arrived(0, g)

        def one(p):
            here = columns(p * piece + g)
            out = of[:, here] + nn(qw[:, here], fin[0, g, p].astype(BF16))
            of[:, here] = out
            scaled = gain_ref[:, here] * cot_ref[:, here].astype(F32)
            stat[0] += out * out
            stat[1] += out * scaled

        loop(nx, one)

    def backward_work(g):
        def one(p):
            h = p * piece + g
            here = columns(h)
            d_out = dob[:, here]
            q, k, v = q_ref[:, here], k_ref[:, here], v_ref[:, here]
            top = (nt(d_out[:half], v[:half]) * mask[h, 0]).astype(BF16)
            bottom = nt(d_out[half:], v)
            low_left = (bottom[:, :half] * mask[h, 1]).astype(BF16)
            low_right = (bottom[:, half:] * mask[h, 2]).astype(BF16)
            entry = fin[0, g, p].astype(BF16)
            weighted = (d_out.astype(F32) * jnp.exp(cc[h])).astype(BF16)
            cross = nt(weighted, entry)
            gq_ref[:half, here] = (nn(top, k[:half]) + cross[:half]).astype(BF16)
            gq_ref[half:, here] = (nn(low_left, k[:half]) + nn(low_right, k[half:]) + cross[half:]).astype(BF16)
            gkf[:half, here] = tn(top, q[:half]) + tn(low_left, q[half:])
            gkf[half:, here] = tn(low_right, q[half:])
            gvf[:half, here] = tn(sc[h, 0], d_out[:half]) + tn(sc[h, 1], d_out[half:])
            gvf[half:, here] = tn(sc[h, 2], d_out[half:])

        loop(nx, one)

    def leave(g):
        arrived(1, g)

        def one(p):
            here = columns(p * piece + g)
            low = fin[1, g, p].astype(BF16)
            gk_ref[:, here] = (gkf[:, here] + nt(vw[:, here], low)).astype(BF16)
            gv_ref[:, here] = (gvf[:, here] + nn(kw[:, here], low)).astype(BF16)

        loop(nx, one)

    def scan(way, tasks, work, last):
        levels = [x_reduce, z_reduce, z_expand, x_expand]
        tasks = list(tasks)
        now = 0.0
        for when, level, c in timetable(chunks):
            while tasks and now + work <= when + SLACK_US:
                tasks.pop(0)()
                now += work
            if level < len(levels):
                levels[level](way, c)
                now = max(now, when) + EVENT_US
            elif c % CUTS == CUTS - 1:
                while tasks:
                    tasks.pop(0)()
                last(c // CUTS)

    def forward_group(g):
        loop(nx, lambda p: forward_work(p * piece + g))

    stat[...] = jnp.zeros_like(stat)
    q_load.wait()
    cot_load.wait()
    gain_load.wait()
    scan(0, [functools.partial(forward_group, g) for g in range(piece)], FORWARD_US * nx, enter)

    ones = jnp.ones((8, DH), F32)
    pick = lax.broadcasted_iota(jnp.int32, (8, rows), 0) < 4
    hs[...] = jnp.where(pick, nt(ones, stat[0], **exact), nt(ones, stat[1], **exact))
    hr[hd] = hs[...]
    h_copies = [push(hs, hr.at[hd], hsend.at[i - 1], hrecv.at[i - 1], h_dev(i)) for i in order(nhd)]
    for copy in h_copies:
        copy.wait_recv()
    both = hr[0]
    for s in range(1, nhd):
        both = both + hr[s]
    features = nhd * q_ref.shape[1]
    square_sum, inner_sum = both[0:1, :], both[4:5, :]
    root_mean = jnp.sqrt(square_sum / features + eps_norm)
    scales = jnp.where(pick, 1.0 / root_mean, inner_sum / (features * root_mean * root_mean * root_mean))
    where = lax.broadcasted_iota(jnp.int32, (8, DH), 0)
    stat[0] = tn(scales, (where == 0).astype(F32), **exact)
    stat[1] = tn(scales, (where == 4).astype(F32), **exact)

    for g in range(piece):
        def one(p, g=g):
            here = columns(p * piece + g)
            scaled = gain_ref[:, here] * cot_ref[:, here].astype(F32)
            d_out = (scaled * stat[0] - of[:, here] * stat[1]).astype(BF16)
            dob[:, here] = d_out
            keep(1, g, p, tn(qw[:, here], d_out))

        loop(nx, one)
        for u in range(CUTS):
            x_send(1, g * CUTS + u)

    def flush(i, src, dst):
        copy = pltpu.make_async_copy(src, dst, out_sem.at[i])
        copy.start()
        return copy

    stores = []

    def end(g):
        if g == 0:
            stores.append(flush(0, gq_ref, gq_out))
            leave_behind(0)
            for level in decay_copies.values():
                for copy in level:
                    copy.wait_send()
            for copy in h_copies:
                copy.wait_send()
        leave(g)
        for p in range(nx):
            h = p * piece + g
            stores.append(flush(1 + 2 * h, gk_ref.at[:, columns(h)], gk_out.at[:, columns(h)]))
            stores.append(flush(2 + 2 * h, gv_ref.at[:, columns(h)], gv_out.at[:, columns(h)]))

    scan(1, [functools.partial(backward_work, g) for g in range(piece)], BACKWARD_US * nx, end)
    leave_behind(1)
    for copy in stores:
        copy.wait()


SLICES = 4


def hand_over(a_in, b_in, c_in, a_out, b_out, c_out, sem):
    copies = []
    for i, (src, dst) in enumerate([(a_in, a_out), (b_in, b_out), (c_in, c_out)]):
        rows = src.shape[0] // SLICES
        for j in range(SLICES):
            part = pl.ds(j * rows, rows)
            copies.append(pltpu.make_async_copy(src.at[part], dst.at[part], sem.at[i, j]))
    for copy in copies:
        copy.start()
    for copy in copies:
        copy.wait()


def shards(dims, queries, key_rows, value_rows, cotangent, log_decay, norm_gain):
    ny, nz, nx, nhd = dims
    rows, width = queries.shape
    heads = log_decay.shape[0]
    piece = heads // nx
    chunks = piece * CUTS
    cut = DH // CUTS
    strip = cut // nz
    half = rows // 2
    vmem = pltpu.VMEM
    dma = pltpu.SemaphoreType.DMA
    most = max(nx, ny, nz) - 1
    scratch = [
        vmem((rows, width), BF16),
        vmem((rows, width), BF16),
        vmem((rows, width), BF16),
        vmem((rows, width), BF16),
        vmem((heads, rows), F32),
        vmem((1, width), F32),
        vmem((rows, width), BF16),
        vmem((rows, width), BF16),
        vmem((rows, width), BF16),
        vmem((heads, rows, DH), F32),
        vmem((heads, rows), F32),
        vmem((rows, width), BF16),
        vmem((rows, width), BF16),
        vmem((rows, width), BF16),
        vmem((heads, 3, half, half), F32),
        vmem((heads, 3, half, half), BF16),
        vmem((rows, width), F32),
        vmem((rows, width), BF16),
        vmem((rows, width), F32),
        vmem((rows, width), F32),
        vmem((2, rows, DH), F32),
        vmem((2, chunks, nx, cut, DH), F32),
        vmem((2, chunks, nx, cut, DH), F32),
        vmem((2, chunks, cut, DH), F32),
        vmem((2, chunks, nz, strip, DH), F32),
        vmem((2, chunks, strip, DH), F32),
        vmem((2, chunks, ny, strip, DH), F32),
        vmem((2, chunks, nz, strip, DH), F32),
        vmem((2, chunks, cut, DH), F32),
        vmem((2, chunks, nx, cut, DH), F32),
        vmem((2, piece, nx, DH, DH), F32),
        vmem((nx, piece, 8, DH), F32),
        vmem((nx, piece, 8, DH), F32),
        vmem((piece, 8, DH), F32),
        vmem((nz, piece, 8, DH), F32),
        vmem((piece, 8, DH), F32),
        vmem((ny, piece, 8, DH), F32),
        vmem((8, rows), F32),
        vmem((nhd, 8, rows), F32),
        dma((2, 5, chunks)),
        dma((2, 5, chunks)),
        dma((3, most)),
        dma((3, most)),
        dma((max(nhd - 1, 1),)),
        dma((max(nhd - 1, 1),)),
        dma((6,)),
        dma((1 + 2 * heads,)),
    ]
    grads = pl.pallas_call(
        functools.partial(kernel, dims),
        out_shape=[jax.ShapeDtypeStruct((rows, width), BF16)] * 3,
        in_specs=[pl.BlockSpec(memory_space=pltpu.HBM)] * 6,
        out_specs=[pl.BlockSpec(memory_space=pl.ANY)] * 3,
        scratch_shapes=scratch,
        compiler_params=pltpu.CompilerParams(
            collective_id=0, has_side_effects=True, vmem_limit_bytes=50 * 1024 * 1024
        ),
    )(queries, key_rows, value_rows, cotangent, log_decay, norm_gain.reshape(1, width))
    return pl.pallas_call(
        hand_over,
        out_shape=[jax.ShapeDtypeStruct((rows, width), BF16)] * 3,
        in_specs=[pl.BlockSpec(memory_space=pl.ANY)] * 3,
        out_specs=[pl.BlockSpec(memory_space=pl.ANY)] * 3,
        scratch_shapes=[dma((3, SLICES))],
        compiler_params=pltpu.CompilerParams(vmem_limit_bytes=8 * 1024 * 1024),
    )(*grads)


def solution(mesh):
    ny, nz, nx = PARTS[mesh.shape["ctx"]]
    dims = (ny, nz, nx, mesh.shape["head"])
    in_specs = (
        P("ctx", "head"),
        P("ctx", "head"),
        P("ctx", "head"),
        P("ctx", "head"),
        P("head", "ctx"),
        P("head"),
    )
    out_specs = (P("ctx", "head"), P("ctx", "head"), P("ctx", "head"))
    return jax.shard_map(
        functools.partial(shards, dims), mesh=mesh, in_specs=in_specs, out_specs=out_specs, check_vma=False
    )
```

```python
import functools

import jax
import jax.numpy as jnp
from jax import lax
from jax.experimental import pallas as pl
from jax.experimental.pallas import tpu as pltpu
from jax.sharding import PartitionSpec as P

eps_norm = 1e-06
MESH = pl.DeviceIdType.MESH
F32, BF16 = jnp.float32, jnp.bfloat16
DH = 128
PARTS = {64: (4, 4, 4), 8: (2, 2, 2)}
X_OUT, Z_OUT, Y_ALL, Z_BACK, X_BACK = range(5)


def nn(a, b, **kw):
    return lax.dot_general(a, b, (((1,), (0,)), ((), ())), preferred_element_type=F32, **kw)


def nt(a, b, **kw):
    return lax.dot_general(a, b, (((1,), (1,)), ((), ())), preferred_element_type=F32, **kw)


def tn(a, b, **kw):
    return lax.dot_general(a, b, (((0,), (0,)), ((), ())), preferred_element_type=F32, **kw)


LATENCY = {"x": 3.5, "z": 4.0, "y": 3.5}
CARRY = {"x": 10.5, "z": 5.2, "y": 1.3}
FORWARD_US, BACKWARD_US, EVENT_US, SLACK_US = 0.22, 0.38, 0.2, 0.3
CUTS = 2


def timetable(chunks):
    free = {}
    events = []
    ready = [0.0] * chunks
    for level, axis in enumerate(["x", "z", "y", "z", "x"]):
        link = axis if level else "x"
        for c in range(chunks):
            begin = max(free.get(link, 0.0), ready[c])
            free[link] = begin + CARRY[axis] / chunks
            ready[c] = free[link] + LATENCY[axis]
            events.append((ready[c], level, c))
    return sorted(events)


def kernel(
    dims, q_in, k_in, v_in, cot_in, ld_in, gain_in, gq_ref, gk_ref, gv_ref,
    q_ref, k_ref, v_ref, cot_ref, ld_ref, gain_ref, cc, crow, kw, vw, qw, mask, sc, of, dob, gkf, gvf, stat,
    st, xr, tz, zr, uy, yr, ez, er, ex, fin,
    xds, xd, zds, zd, yds, yd, hs, hr,
    send_sem, recv_sem, dsend, drecv, hsend, hrecv, in_sem,
):
    ny, nz, nx, nhd = dims
    rows = q_ref.shape[0]
    half = rows // 2
    heads = ld_ref.shape[0]
    piece = heads // nx
    chunks = piece * CUTS
    cut = DH // CUTS
    strip = cut // nz
    exact = dict(precision=lax.Precision.HIGHEST)

    me = lax.axis_index("ctx")
    hd = lax.axis_index("head")
    x = lax.rem(me, nx)
    z = lax.rem(lax.div(me, nx), nz)
    y = lax.div(me, nx * nz)

    def x_at(i):
        return lax.rem(x + i, nx)

    def z_at(i):
        return lax.rem(z + i, nz)

    def y_at(i):
        return lax.rem(y + i, ny)

    def x_dev(i):
        return {"ctx": me - x + x_at(i), "head": hd}

    def z_dev(i):
        return {"ctx": me + (z_at(i) - z) * nx, "head": hd}

    def y_dev(i):
        return {"ctx": me + (y_at(i) - y) * (nx * nz), "head": hd}

    def h_dev(i):
        return {"ctx": me, "head": lax.rem(hd + i, nhd)}

    partners = (
        [x_dev(i) for i in range(1, nx)] + [z_dev(i) for i in range(1, nz)]
        + [y_dev(i) for i in range(1, ny)] + [h_dev(i) for i in range(1, nhd)]
    )
    barrier = pltpu.get_barrier_semaphore()
    for device in partners:
        pl.semaphore_signal(barrier, inc=1, device_id=device, device_id_type=MESH)

    def load(i, src, dst):
        copy = pltpu.make_async_copy(src, dst, in_sem.at[i])
        copy.start()
        return copy

    ld_load = load(0, ld_in, ld_ref)
    k_load = load(1, k_in, k_ref)
    v_load = load(2, v_in, v_ref)
    q_load = load(3, q_in, q_ref)
    cot_load = load(4, cot_in, cot_ref)
    gain_load = load(5, gain_in, gain_ref)

    def push(src, dst, send, recv, device):
        copy = pltpu.make_async_remote_copy(
            src_ref=src, dst_ref=dst, send_sem=send, recv_sem=recv, device_id=device, device_id_type=MESH
        )
        copy.start()
        return copy

    def columns(h):
        if isinstance(h, int):
            return pl.ds(h * DH, DH)
        return pl.ds(pl.multiple_of(h * DH, DH), DH)

    def order(count):
        return sorted(range(1, count), key=lambda i: -min(i, count - i))

    ld_load.wait()
    ld = ld_ref[...]
    r_i = lax.broadcasted_iota(jnp.int32, (rows, rows), 0)
    c_i = lax.broadcasted_iota(jnp.int32, (rows, rows), 1)
    crow[...] = nn(ld, (r_i <= c_i).astype(F32), **exact)
    cum_t = nt((r_i >= c_i).astype(F32), ld, **exact)
    end_t = cum_t[rows - 1:rows, :]
    bg_t = jnp.exp(end_t - cum_t)
    fall_t = jnp.exp(end_t)
    for h in range(heads):
        cc[h] = jnp.broadcast_to(cum_t[:, h:h + 1], (rows, DH))
        xds[h // piece, h % piece] = jnp.broadcast_to(fall_t[:, h:h + 1], (8, DH))

    xd[x] = xds[x]

    def x_send(way, c):
        for i in order(nx):
            push(
                st.at[way, c, x_at(i)], xr.at[way, c, x],
                send_sem.at[way, X_OUT, c], recv_sem.at[way, X_OUT, c], x_dev(i),
            )
        xr[way, c, x] = st[way, c, x]

    def arrive(way, level, c):
        size = sizes(level, way, c)
        pltpu.make_async_copy(size, size, recv_sem.at[way, level, c]).wait()

    def leave_behind(way):
        for level in range(5):
            for c in range(chunks):
                size = sizes(level, way, c)
                pltpu.make_async_copy(size, size, send_sem.at[way, level, c]).wait()

    def sizes(level, way, c):
        if level in (X_OUT, X_BACK):
            return xr.at[way, c, pl.ds(0, nx - 1)]
        return (zr if level in (Z_OUT, Z_BACK) else yr).at[way, c, pl.ds(0, (ny if level == Y_ALL else nz) - 1)]

    def along(way, count):
        return range(count) if way == 0 else range(count - 1, -1, -1)

    def keep(way, g, p, state):
        for u in range(CUTS):
            st[way, g * CUTS + u, p] = state[u * cut:(u + 1) * cut]

    k_load.wait()
    v_load.wait()
    decay_copies = {}
    for g in range(piece):
        for p in range(nx):
            h = p * piece + g
            back = jnp.broadcast_to(bg_t[:, h:h + 1], (rows, DH))
            weighted = (k_ref[:, columns(h)].astype(F32) * back).astype(BF16)
            kw[:, columns(h)] = weighted
            keep(0, g, p, tn(weighted, v_ref[:, columns(h)]))
        if g == 0:
            pl.semaphore_wait(barrier, len(partners))
            decay_copies[X_OUT] = [
                push(xds.at[x_at(i)], xd.at[x], dsend.at[0, i - 1], drecv.at[0, i - 1], x_dev(i)) for i in order(nx)
            ]
        for u in range(CUTS):
            x_send(0, g * CUTS + u)

    def z_decays():
        for copy in decay_copies[X_OUT]:
            copy.wait_recv()
        total = xd[0]
        for s in range(1, nx):
            total = total * xd[s]
        zds[...] = total
        zd[z] = total
        decay_copies[Z_OUT] = [
            push(zds, zd.at[z], dsend.at[1, i - 1], drecv.at[1, i - 1], z_dev(i)) for i in order(nz)
        ]

    def y_decays():
        for copy in decay_copies[Z_OUT]:
            copy.wait_recv()
        total = zd[0]
        for s in range(1, nz):
            total = total * zd[s]
        yds[...] = total
        yd[y] = total
        decay_copies[Y_ALL] = [
            push(yds, yd.at[y], dsend.at[2, i - 1], drecv.at[2, i - 1], y_dev(i)) for i in order(ny)
        ]

    def x_reduce(way, c):
        g = c // CUTS
        if way == 0 and c == 0:
            z_decays()
        arrive(way, X_OUT, c)
        path = list(along(way, nx))
        total = xr[way, c, path[0]]
        for s in path[1:]:
            total = xd[s, g, 0:1, :] * total + xr[way, c, s]
        tz[way, c] = total
        for i in order(nz):
            push(
                tz.at[way, c, pl.ds(z_at(i) * strip, strip)], zr.at[way, c, z],
                send_sem.at[way, Z_OUT, c], recv_sem.at[way, Z_OUT, c], z_dev(i),
            )
        zr[way, c, z] = tz[way, c, pl.ds(z * strip, strip)]

    def z_reduce(way, c):
        g = c // CUTS
        if way == 0 and c == 0:
            y_decays()
        arrive(way, Z_OUT, c)
        path = list(along(way, nz))
        total = zr[way, c, path[0]]
        for s in path[1:]:
            total = zd[s, g, 0:1, :] * total + zr[way, c, s]
        uy[way, c] = total
        for i in order(ny):
            push(
                uy.at[way, c], yr.at[way, c, y],
                send_sem.at[way, Y_ALL, c], recv_sem.at[way, Y_ALL, c], y_dev(i),
            )
        yr[way, c, y] = total

    def z_expand(way, c):
        g = c // CUTS
        if way == 0 and c == 0:
            for copy in decay_copies[Y_ALL]:
                copy.wait_recv()
        arrive(way, Y_ALL, c)
        state = jnp.zeros((strip, DH), F32)
        for s in along(way, ny):
            longer = yd[s, g, 0:1, :] * state + yr[way, c, s]
            before = (s < y) if way == 0 else (s > y)
            state = jnp.where(before, longer, state)
        for s in along(way, nz):
            ez[way, c, s] = state
            state = zd[s, g, 0:1, :] * state + zr[way, c, s]
        for i in order(nz):
            push(
                ez.at[way, c, z_at(i)], er.at[way, c, pl.ds(z * strip, strip)],
                send_sem.at[way, Z_BACK, c], recv_sem.at[way, Z_BACK, c], z_dev(i),
            )
        er[way, c, pl.ds(z * strip, strip)] = ez[way, c, z]

    def x_expand(way, c):
        g, u = c // CUTS, c % CUTS
        arrive(way, Z_BACK, c)
        state = er[way, c]
        for s in along(way, nx):
            ex[way, c, s] = state
            state = xd[s, g, 0:1, :] * state + xr[way, c, s]
        here = pl.ds(u * cut, cut)
        for i in order(nx):
            push(
                ex.at[way, c, x_at(i)], fin.at[way, g, x, here],
                send_sem.at[way, X_BACK, c], recv_sem.at[way, X_BACK, c], x_dev(i),
            )
        fin[way, g, x, here] = ex[way, c, x]

    def arrived(way, g):
        for u in range(CUTS):
            arrive(way, X_BACK, g * CUTS + u)

    def loop(count, body):
        pair = 2 if count % 2 == 0 else 1

        def step(j, carry):
            for u in range(pair):
                body(j * pair + u)
            return carry

        lax.fori_loop(0, count // pair, step, 0)

    lower = (
        lax.broadcasted_iota(jnp.int32, (half, half), 0) >= lax.broadcasted_iota(jnp.int32, (half, half), 1)
    )

    def forward_work(h):
        here = columns(h)
        col = cc[h]
        line = crow[pl.ds(h, 1), :]
        m00 = jnp.where(lower, jnp.exp(jnp.minimum(col[:half] - line[:, :half], 0.0)), 0.0)
        m10 = jnp.exp(jnp.minimum(col[half:] - line[:, :half], 0.0))
        m11 = jnp.where(lower, jnp.exp(jnp.minimum(col[half:] - line[:, half:], 0.0)), 0.0)
        mask[h, 0], mask[h, 1], mask[h, 2] = m00, m10, m11
        q, k, v = q_ref[:, here], k_ref[:, here], v_ref[:, here]
        top = (nt(q[:half], k[:half]) * m00).astype(BF16)
        bottom = nt(q[half:], k)
        low_left = (bottom[:, :half] * m10).astype(BF16)
        low_right = (bottom[:, half:] * m11).astype(BF16)
        sc[h, 0], sc[h, 1], sc[h, 2] = top, low_left, low_right
        of[:half, here] = nn(top, v[:half])
        of[half:, here] = nn(low_left, v[:half]) + nn(low_right, v[half:])
        qw[:, here] = (q.astype(F32) * jnp.exp(col)).astype(BF16)
        vw[:, here] = (v.astype(F32) * jnp.exp(col[rows - 1:rows, :] - col)).astype(BF16)

    def enter(g):
        arrived(0, g)

        def one(p):
            here = columns(p * piece + g)
            out = of[:, here] + nn(qw[:, here], fin[0, g, p].astype(BF16))
            of[:, here] = out
            scaled = gain_ref[:, here] * cot_ref[:, here].astype(F32)
            stat[0] += out * out
            stat[1] += out * scaled

        loop(nx, one)

    def backward_work(h):
        here = columns(h)
        d_out = dob[:, here]
        q, k, v = q_ref[:, here], k_ref[:, here], v_ref[:, here]
        top = (nt(d_out[:half], v[:half]) * mask[h, 0]).astype(BF16)
        bottom = nt(d_out[half:], v)
        low_left = (bottom[:, :half] * mask[h, 1]).astype(BF16)
        low_right = (bottom[:, half:] * mask[h, 2]).astype(BF16)
        entry = fin[0, lax.rem(h, piece), lax.div(h, piece)].astype(BF16)
        weighted = (d_out.astype(F32) * jnp.exp(cc[h])).astype(BF16)
        cross = nt(weighted, entry)
        gq_ref[:half, here] = (nn(top, k[:half]) + cross[:half]).astype(BF16)
        gq_ref[half:, here] = (nn(low_left, k[:half]) + nn(low_right, k[half:]) + cross[half:]).astype(BF16)
        gkf[:half, here] = tn(top, q[:half]) + tn(low_left, q[half:])
        gkf[half:, here] = tn(low_right, q[half:])
        gvf[:half, here] = tn(sc[h, 0], d_out[:half]) + tn(sc[h, 1], d_out[half:])
        gvf[half:, here] = tn(sc[h, 2], d_out[half:])

    def leave(g):
        arrived(1, g)

        def one(p):
            here = columns(p * piece + g)
            low = fin[1, g, p].astype(BF16)
            gk_ref[:, here] = (gkf[:, here] + nt(vw[:, here], low)).astype(BF16)
            gv_ref[:, here] = (gvf[:, here] + nn(kw[:, here], low)).astype(BF16)

        loop(nx, one)

    def scan(way, tasks, work, last):
        levels = [x_reduce, z_reduce, z_expand, x_expand]
        tasks = list(tasks)
        now = 0.0
        for when, level, c in timetable(chunks):
            if level < len(levels):
                while tasks and now + work <= when + SLACK_US:
                    tasks.pop(0)()
                    now += work
                levels[level](way, c)
                now = max(now, when) + EVENT_US
        for task in tasks:
            task()
        for g in range(piece):
            last(g)

    def some(work):
        return [functools.partial(loop, 2, lambda u, j=j: work(2 * j + u)) for j in range(heads // 2)]

    stat[...] = jnp.zeros_like(stat)
    q_load.wait()
    cot_load.wait()
    gain_load.wait()
    scan(0, some(forward_work), FORWARD_US * 2, enter)

    ones = jnp.ones((8, DH), F32)
    pick = lax.broadcasted_iota(jnp.int32, (8, rows), 0) < 4
    hs[...] = jnp.where(pick, nt(ones, stat[0], **exact), nt(ones, stat[1], **exact))
    hr[hd] = hs[...]
    h_copies = [push(hs, hr.at[hd], hsend.at[i - 1], hrecv.at[i - 1], h_dev(i)) for i in order(nhd)]
    for copy in h_copies:
        copy.wait_recv()
    both = hr[0]
    for s in range(1, nhd):
        both = both + hr[s]
    features = nhd * q_ref.shape[1]
    square_sum, inner_sum = both[0:1, :], both[4:5, :]
    root_mean = jnp.sqrt(square_sum / features + eps_norm)
    scales = jnp.where(pick, 1.0 / root_mean, inner_sum / (features * root_mean * root_mean * root_mean))
    where = lax.broadcasted_iota(jnp.int32, (8, DH), 0)
    stat[0] = tn(scales, (where == 0).astype(F32), **exact)
    stat[1] = tn(scales, (where == 4).astype(F32), **exact)

    for g in range(piece):
        def one(p, g=g):
            here = columns(p * piece + g)
            scaled = gain_ref[:, here] * cot_ref[:, here].astype(F32)
            d_out = (scaled * stat[0] - of[:, here] * stat[1]).astype(BF16)
            dob[:, here] = d_out
            keep(1, g, p, tn(qw[:, here], d_out))

        loop(nx, one)
        for u in range(CUTS):
            x_send(1, g * CUTS + u)

    def end(g):
        if g == 0:
            leave_behind(0)
            for level in decay_copies.values():
                for copy in level:
                    copy.wait_send()
            for copy in h_copies:
                copy.wait_send()
        leave(g)

    scan(1, some(backward_work), BACKWARD_US * 2, end)
    leave_behind(1)


SLICES = 4


def hand_over(a_in, b_in, c_in, a_out, b_out, c_out, sem):
    copies = []
    for i, (src, dst) in enumerate([(a_in, a_out), (b_in, b_out), (c_in, c_out)]):
        rows = src.shape[0] // SLICES
        for j in range(SLICES):
            part = pl.ds(j * rows, rows)
            copies.append(pltpu.make_async_copy(src.at[part], dst.at[part], sem.at[i, j]))
    for copy in copies:
        copy.start()
    for copy in copies:
        copy.wait()


def shards(dims, queries, key_rows, value_rows, cotangent, log_decay, norm_gain):
    ny, nz, nx, nhd = dims
    rows, width = queries.shape
    heads = log_decay.shape[0]
    piece = heads // nx
    chunks = piece * CUTS
    cut = DH // CUTS
    strip = cut // nz
    half = rows // 2
    vmem = pltpu.VMEM
    dma = pltpu.SemaphoreType.DMA
    most = max(nx, ny, nz) - 1
    scratch = [
        vmem((rows, width), BF16),
        vmem((rows, width), BF16),
        vmem((rows, width), BF16),
        vmem((rows, width), BF16),
        vmem((heads, rows), F32),
        vmem((1, width), F32),
        vmem((heads, rows, DH), F32),
        vmem((heads, rows), F32),
        vmem((rows, width), BF16),
        vmem((rows, width), BF16),
        vmem((rows, width), BF16),
        vmem((heads, 3, half, half), F32),
        vmem((heads, 3, half, half), BF16),
        vmem((rows, width), F32),
        vmem((rows, width), BF16),
        vmem((rows, width), F32),
        vmem((rows, width), F32),
        vmem((2, rows, DH), F32),
        vmem((2, chunks, nx, cut, DH), F32),
        vmem((2, chunks, nx, cut, DH), F32),
        vmem((2, chunks, cut, DH), F32),
        vmem((2, chunks, nz, strip, DH), F32),
        vmem((2, chunks, strip, DH), F32),
        vmem((2, chunks, ny, strip, DH), F32),
        vmem((2, chunks, nz, strip, DH), F32),
        vmem((2, chunks, cut, DH), F32),
        vmem((2, chunks, nx, cut, DH), F32),
        vmem((2, piece, nx, DH, DH), F32),
        vmem((nx, piece, 8, DH), F32),
        vmem((nx, piece, 8, DH), F32),
        vmem((piece, 8, DH), F32),
        vmem((nz, piece, 8, DH), F32),
        vmem((piece, 8, DH), F32),
        vmem((ny, piece, 8, DH), F32),
        vmem((8, rows), F32),
        vmem((nhd, 8, rows), F32),
        dma((2, 5, chunks)),
        dma((2, 5, chunks)),
        dma((3, most)),
        dma((3, most)),
        dma((max(nhd - 1, 1),)),
        dma((max(nhd - 1, 1),)),
        dma((6,)),
    ]
    grads = pl.pallas_call(
        functools.partial(kernel, dims),
        out_shape=[pltpu.VMEM((rows, width), BF16)] * 3,
        in_specs=[pl.BlockSpec(memory_space=pltpu.HBM)] * 6,
        out_specs=[pl.BlockSpec(memory_space=pltpu.VMEM)] * 3,
        scratch_shapes=scratch,
        compiler_params=pltpu.CompilerParams(
            collective_id=0, has_side_effects=True, vmem_limit_bytes=50 * 1024 * 1024
        ),
    )(*(
        pltpu.with_memory_space_constraint(array, pltpu.HBM)
        for array in (queries, key_rows, value_rows, cotangent, log_decay, norm_gain.reshape(1, width))
    ))
    return pl.pallas_call(
        hand_over,
        out_shape=[jax.ShapeDtypeStruct((rows, width), BF16)] * 3,
        in_specs=[pl.BlockSpec(memory_space=pl.ANY)] * 3,
        out_specs=[pl.BlockSpec(memory_space=pl.ANY)] * 3,
        scratch_shapes=[dma((3, SLICES))],
        compiler_params=pltpu.CompilerParams(vmem_limit_bytes=8 * 1024 * 1024),
    )(*grads)


def solution(mesh):
    ny, nz, nx = PARTS[mesh.shape["ctx"]]
    dims = (ny, nz, nx, mesh.shape["head"])
    in_specs = (
        P("ctx", "head"),
        P("ctx", "head"),
        P("ctx", "head"),
        P("ctx", "head"),
        P("head", "ctx"),
        P("head"),
    )
    out_specs = (P("ctx", "head"), P("ctx", "head"), P("ctx", "head"))
    return jax.shard_map(
        functools.partial(shards, dims), mesh=mesh, in_specs=in_specs, out_specs=out_specs, check_vma=False
    )
```

```python
import functools

import jax
import jax.numpy as jnp
from jax import lax
from jax.experimental import pallas as pl
from jax.experimental.pallas import tpu as pltpu
from jax.sharding import PartitionSpec as P

eps_norm = 1e-06
MESH = pl.DeviceIdType.MESH
F32, BF16 = jnp.float32, jnp.bfloat16
DH = 128
PARTS = {64: (4, 4, 4), 8: (2, 2, 2)}
X_OUT, Z_OUT, Y_ALL, Z_BACK, X_BACK = range(5)


def nn(a, b, **kw):
    return lax.dot_general(a, b, (((1,), (0,)), ((), ())), preferred_element_type=F32, **kw)


def nt(a, b, **kw):
    return lax.dot_general(a, b, (((1,), (1,)), ((), ())), preferred_element_type=F32, **kw)


def tn(a, b, **kw):
    return lax.dot_general(a, b, (((0,), (0,)), ((), ())), preferred_element_type=F32, **kw)


LATENCY = {"x": 3.5, "z": 4.0, "y": 3.5}
CARRY = {"x": 10.5, "z": 5.2, "y": 1.3}
FORWARD_US, BACKWARD_US, EVENT_US, SLACK_US = 0.22, 0.38, 0.2, 0.3
CUTS = 2


def timetable(chunks):
    free = {}
    events = []
    ready = [0.0] * chunks
    for level, axis in enumerate(["x", "z", "y", "z", "x"]):
        link = axis if level else "x"
        for c in range(chunks):
            begin = max(free.get(link, 0.0), ready[c])
            free[link] = begin + CARRY[axis] / chunks
            ready[c] = free[link] + LATENCY[axis]
            events.append((ready[c], level, c))
    return sorted(events)


def kernel(
    dims, q_in, k_in, v_in, cot_in, ld_in, gain_in, gq_ref, gk_ref, gv_ref,
    q_ref, k_ref, v_ref, cot_ref, ld_ref, gain_ref, cc, crow, kw, vw, qw, mask, sc, of, dob, gkf, gvf, stat,
    st, xr, tz, zr, uy, yr, ez, er, ex, fin,
    xds, xd, zds, zd, yds, yd, hs, hr,
    send_sem, recv_sem, dsend, drecv, hsend, hrecv, in_sem,
):
    ny, nz, nx, nhd = dims
    rows = q_ref.shape[0]
    half = rows // 2
    heads = ld_ref.shape[0]
    piece = heads // nx
    chunks = piece * CUTS
    cut = DH // CUTS
    strip = cut // nz
    exact = dict(precision=lax.Precision.HIGHEST)

    me = lax.axis_index("ctx")
    hd = lax.axis_index("head")
    x = lax.rem(me, nx)
    z = lax.rem(lax.div(me, nx), nz)
    y = lax.div(me, nx * nz)

    def x_at(i):
        return lax.rem(x + i, nx)

    def z_at(i):
        return lax.rem(z + i, nz)

    def y_at(i):
        return lax.rem(y + i, ny)

    def x_dev(i):
        return {"ctx": me - x + x_at(i), "head": hd}

    def z_dev(i):
        return {"ctx": me + (z_at(i) - z) * nx, "head": hd}

    def y_dev(i):
        return {"ctx": me + (y_at(i) - y) * (nx * nz), "head": hd}

    def h_dev(i):
        return {"ctx": me, "head": lax.rem(hd + i, nhd)}

    partners = (
        [x_dev(i) for i in range(1, nx)] + [z_dev(i) for i in range(1, nz)]
        + [y_dev(i) for i in range(1, ny)] + [h_dev(i) for i in range(1, nhd)]
    )
    barrier = pltpu.get_barrier_semaphore()
    for device in partners:
        pl.semaphore_signal(barrier, inc=1, device_id=device, device_id_type=MESH)

    def load(i, src, dst):
        copy = pltpu.make_async_copy(src, dst, in_sem.at[i])
        copy.start()
        return copy

    ld_load = load(0, ld_in, ld_ref)
    k_load = load(1, k_in, k_ref)
    v_load = load(2, v_in, v_ref)
    q_load = load(3, q_in, q_ref)
    cot_load = load(4, cot_in, cot_ref)
    gain_load = load(5, gain_in, gain_ref)

    def push(src, dst, send, recv, device):
        copy = pltpu.make_async_remote_copy(
            src_ref=src, dst_ref=dst, send_sem=send, recv_sem=recv, device_id=device, device_id_type=MESH
        )
        copy.start()
        return copy

    def columns(h):
        if isinstance(h, int):
            return pl.ds(h * DH, DH)
        return pl.ds(pl.multiple_of(h * DH, DH), DH)

    def order(count):
        return sorted(range(1, count), key=lambda i: -min(i, count - i))

    ld_load.wait()
    ld = ld_ref[...]
    r_i = lax.broadcasted_iota(jnp.int32, (rows, rows), 0)
    c_i = lax.broadcasted_iota(jnp.int32, (rows, rows), 1)
    crow[...] = nn(ld, (r_i <= c_i).astype(F32), **exact)
    cum_t = nt((r_i >= c_i).astype(F32), ld, **exact)
    end_t = cum_t[rows - 1:rows, :]
    bg_t = jnp.exp(end_t - cum_t)
    fall_t = jnp.exp(end_t)
    for h in range(heads):
        cc[h] = jnp.broadcast_to(cum_t[:, h:h + 1], (rows, DH))
        xds[h // piece, h % piece] = jnp.broadcast_to(fall_t[:, h:h + 1], (8, DH))

    xd[x] = xds[x]

    def x_send(way, c):
        for i in order(nx):
            push(
                st.at[way, c, x_at(i)], xr.at[way, c, x],
                send_sem.at[way, X_OUT, c], recv_sem.at[way, X_OUT, c], x_dev(i),
            )
        xr[way, c, x] = st[way, c, x]

    def arrive(way, level, c):
        size = sizes(level, way, c)
        pltpu.make_async_copy(size, size, recv_sem.at[way, level, c]).wait()

    def leave_behind(way):
        for level in range(5):
            for c in range(chunks):
                size = sizes(level, way, c)
                pltpu.make_async_copy(size, size, send_sem.at[way, level, c]).wait()

    def sizes(level, way, c):
        if level in (X_OUT, X_BACK):
            return xr.at[way, c, pl.ds(0, nx - 1)]
        return (zr if level in (Z_OUT, Z_BACK) else yr).at[way, c, pl.ds(0, (ny if level == Y_ALL else nz) - 1)]

    def along(way, count):
        return range(count) if way == 0 else range(count - 1, -1, -1)

    def keep(way, g, p, state):
        for u in range(CUTS):
            st[way, g * CUTS + u, p] = state[u * cut:(u + 1) * cut]

    k_load.wait()
    v_load.wait()
    decay_copies = {}
    for g in range(piece):
        for p in range(nx):
            h = p * piece + g
            back = jnp.broadcast_to(bg_t[:, h:h + 1], (rows, DH))
            weighted = (k_ref[:, columns(h)].astype(F32) * back).astype(BF16)
            kw[:, columns(h)] = weighted
            keep(0, g, p, tn(weighted, v_ref[:, columns(h)]))
        if g == 0:
            pl.semaphore_wait(barrier, len(partners))
            decay_copies[X_OUT] = [
                push(xds.at[x_at(i)], xd.at[x], dsend.at[0, i - 1], drecv.at[0, i - 1], x_dev(i)) for i in order(nx)
            ]
        for u in range(CUTS):
            x_send(0, g * CUTS + u)

    def z_decays():
        for copy in decay_copies[X_OUT]:
            copy.wait_recv()
        total = xd[0]
        for s in range(1, nx):
            total = total * xd[s]
        zds[...] = total
        zd[z] = total
        decay_copies[Z_OUT] = [
            push(zds, zd.at[z], dsend.at[1, i - 1], drecv.at[1, i - 1], z_dev(i)) for i in order(nz)
        ]

    def y_decays():
        for copy in decay_copies[Z_OUT]:
            copy.wait_recv()
        total = zd[0]
        for s in range(1, nz):
            total = total * zd[s]
        yds[...] = total
        yd[y] = total
        decay_copies[Y_ALL] = [
            push(yds, yd.at[y], dsend.at[2, i - 1], drecv.at[2, i - 1], y_dev(i)) for i in order(ny)
        ]

    def x_reduce(way, c):
        g = c // CUTS
        if way == 0 and c == 0:
            z_decays()
        arrive(way, X_OUT, c)
        path = list(along(way, nx))
        total = xr[way, c, path[0]]
        for s in path[1:]:
            total = xd[s, g, 0:1, :] * total + xr[way, c, s]
        tz[way, c] = total
        for i in order(nz):
            push(
                tz.at[way, c, pl.ds(z_at(i) * strip, strip)], zr.at[way, c, z],
                send_sem.at[way, Z_OUT, c], recv_sem.at[way, Z_OUT, c], z_dev(i),
            )
        zr[way, c, z] = tz[way, c, pl.ds(z * strip, strip)]

    def z_reduce(way, c):
        g = c // CUTS
        if way == 0 and c == 0:
            y_decays()
        arrive(way, Z_OUT, c)
        path = list(along(way, nz))
        total = zr[way, c, path[0]]
        for s in path[1:]:
            total = zd[s, g, 0:1, :] * total + zr[way, c, s]
        uy[way, c] = total
        for i in order(ny):
            push(
                uy.at[way, c], yr.at[way, c, y],
                send_sem.at[way, Y_ALL, c], recv_sem.at[way, Y_ALL, c], y_dev(i),
            )
        yr[way, c, y] = total

    def z_expand(way, c):
        g = c // CUTS
        if way == 0 and c == 0:
            for copy in decay_copies[Y_ALL]:
                copy.wait_recv()
        arrive(way, Y_ALL, c)
        state = jnp.zeros((strip, DH), F32)
        for s in along(way, ny):
            longer = yd[s, g, 0:1, :] * state + yr[way, c, s]
            before = (s < y) if way == 0 else (s > y)
            state = jnp.where(before, longer, state)
        for s in along(way, nz):
            ez[way, c, s] = state
            state = zd[s, g, 0:1, :] * state + zr[way, c, s]
        for i in order(nz):
            push(
                ez.at[way, c, z_at(i)], er.at[way, c, pl.ds(z * strip, strip)],
                send_sem.at[way, Z_BACK, c], recv_sem.at[way, Z_BACK, c], z_dev(i),
            )
        er[way, c, pl.ds(z * strip, strip)] = ez[way, c, z]

    def x_expand(way, c):
        g, u = c // CUTS, c % CUTS
        arrive(way, Z_BACK, c)
        state = er[way, c]
        for s in along(way, nx):
            ex[way, c, s] = state
            state = xd[s, g, 0:1, :] * state + xr[way, c, s]
        here = pl.ds(u * cut, cut)
        for i in order(nx):
            push(
                ex.at[way, c, x_at(i)], fin.at[way, g, x, here],
                send_sem.at[way, X_BACK, c], recv_sem.at[way, X_BACK, c], x_dev(i),
            )
        fin[way, g, x, here] = ex[way, c, x]

    def arrived(way, g):
        for u in range(CUTS):
            arrive(way, X_BACK, g * CUTS + u)

    def loop(count, body):
        pair = next(size for size in (4, 2, 1) if count % size == 0)

        def step(j, carry):
            for u in range(pair):
                body(j * pair + u)
            return carry

        lax.fori_loop(0, count // pair, step, 0)

    lower = (
        lax.broadcasted_iota(jnp.int32, (half, half), 0) >= lax.broadcasted_iota(jnp.int32, (half, half), 1)
    )

    def forward_work(h):
        here = columns(h)
        col = cc[h]
        line = crow[pl.ds(h, 1), :]
        m00 = jnp.where(lower, jnp.exp(jnp.minimum(col[:half] - line[:, :half], 0.0)), 0.0)
        m10 = jnp.exp(jnp.minimum(col[half:] - line[:, :half], 0.0))
        m11 = jnp.where(lower, jnp.exp(jnp.minimum(col[half:] - line[:, half:], 0.0)), 0.0)
        mask[h, 0], mask[h, 1], mask[h, 2] = m00, m10, m11
        q, k, v = q_ref[:, here], k_ref[:, here], v_ref[:, here]
        top = (nt(q[:half], k[:half]) * m00).astype(BF16)
        bottom = nt(q[half:], k)
        low_left = (bottom[:, :half] * m10).astype(BF16)
        low_right = (bottom[:, half:] * m11).astype(BF16)
        sc[h, 0], sc[h, 1], sc[h, 2] = top, low_left, low_right
        of[:half, here] = nn(top, v[:half])
        of[half:, here] = nn(low_left, v[:half]) + nn(low_right, v[half:])
        qw[:, here] = (q.astype(F32) * jnp.exp(col)).astype(BF16)
        vw[:, here] = (v.astype(F32) * jnp.exp(col[rows - 1:rows, :] - col)).astype(BF16)

    def enter(g):
        arrived(0, g)

        squares, inners = stat[0], stat[1]
        for p in range(nx):
            here = columns(p * piece + g)
            out = of[:, here] + nn(qw[:, here], fin[0, g, p].astype(BF16))
            of[:, here] = out
            squares += out * out
            inners += out * (gain_ref[:, here] * cot_ref[:, here].astype(F32))
        stat[0], stat[1] = squares, inners

    def backward_work(h):
        here = columns(h)
        d_out = dob[:, here]
        q, k, v = q_ref[:, here], k_ref[:, here], v_ref[:, here]
        top = (nt(d_out[:half], v[:half]) * mask[h, 0]).astype(BF16)
        bottom = nt(d_out[half:], v)
        low_left = (bottom[:, :half] * mask[h, 1]).astype(BF16)
        low_right = (bottom[:, half:] * mask[h, 2]).astype(BF16)
        entry = fin[0, lax.rem(h, piece), lax.div(h, piece)].astype(BF16)
        weighted = (d_out.astype(F32) * jnp.exp(cc[h])).astype(BF16)
        cross = nt(weighted, entry)
        gq_ref[:half, here] = (nn(top, k[:half]) + cross[:half]).astype(BF16)
        gq_ref[half:, here] = (nn(low_left, k[:half]) + nn(low_right, k[half:]) + cross[half:]).astype(BF16)
        gkf[:half, here] = tn(top, q[:half]) + tn(low_left, q[half:])
        gkf[half:, here] = tn(low_right, q[half:])
        gvf[:half, here] = tn(sc[h, 0], d_out[:half]) + tn(sc[h, 1], d_out[half:])
        gvf[half:, here] = tn(sc[h, 2], d_out[half:])

    def leave(g):
        arrived(1, g)

        def one(p):
            here = columns(p * piece + g)
            low = fin[1, g, p].astype(BF16)
            gk_ref[:, here] = (gkf[:, here] + nt(vw[:, here], low)).astype(BF16)
            gv_ref[:, here] = (gvf[:, here] + nn(kw[:, here], low)).astype(BF16)

        loop(nx, one)

    def scan(way, tasks, work, last):
        levels = [x_reduce, z_reduce, z_expand, x_expand]
        tasks = list(tasks)
        now = 0.0
        for when, level, c in timetable(chunks):
            if level < len(levels):
                while tasks and now + work <= when + SLACK_US:
                    tasks.pop(0)()
                    now += work
                levels[level](way, c)
                now = max(now, when) + EVENT_US
        for task in tasks:
            task()
        for g in range(piece):
            last(g)

    def some(work):
        return [functools.partial(loop, 2, lambda u, j=j: work(2 * j + u)) for j in range(heads // 2)]

    stat[...] = jnp.zeros_like(stat)
    q_load.wait()
    cot_load.wait()
    gain_load.wait()
    scan(0, some(forward_work), FORWARD_US * 2, enter)

    ones = jnp.ones((8, DH), F32)
    pick = lax.broadcasted_iota(jnp.int32, (8, rows), 0) < 4
    hs[...] = jnp.where(pick, nt(ones, stat[0], **exact), nt(ones, stat[1], **exact))
    hr[hd] = hs[...]
    h_copies = [push(hs, hr.at[hd], hsend.at[i - 1], hrecv.at[i - 1], h_dev(i)) for i in order(nhd)]
    for copy in h_copies:
        copy.wait_recv()
    both = hr[0]
    for s in range(1, nhd):
        both = both + hr[s]
    features = nhd * q_ref.shape[1]
    square_sum, inner_sum = both[0:1, :], both[4:5, :]
    root_mean = jnp.sqrt(square_sum / features + eps_norm)
    scales = jnp.where(pick, 1.0 / root_mean, inner_sum / (features * root_mean * root_mean * root_mean))
    where = lax.broadcasted_iota(jnp.int32, (8, DH), 0)
    stat[0] = tn(scales, (where == 0).astype(F32), **exact)
    stat[1] = tn(scales, (where == 4).astype(F32), **exact)

    for g in range(piece):
        def one(p, g=g):
            here = columns(p * piece + g)
            scaled = gain_ref[:, here] * cot_ref[:, here].astype(F32)
            d_out = (scaled * stat[0] - of[:, here] * stat[1]).astype(BF16)
            dob[:, here] = d_out
            keep(1, g, p, tn(qw[:, here], d_out))

        loop(nx, one)
        for u in range(CUTS):
            x_send(1, g * CUTS + u)

    def end(g):
        if g == 0:
            leave_behind(0)
            for level in decay_copies.values():
                for copy in level:
                    copy.wait_send()
            for copy in h_copies:
                copy.wait_send()
        leave(g)

    scan(1, some(backward_work), BACKWARD_US * 2, end)
    leave_behind(1)


SLICES = 4


def hand_over(a_in, b_in, c_in, a_out, b_out, c_out, sem):
    copies = []
    for i, (src, dst) in enumerate([(a_in, a_out), (b_in, b_out), (c_in, c_out)]):
        rows = src.shape[0] // SLICES
        for j in range(SLICES):
            part = pl.ds(j * rows, rows)
            copies.append(pltpu.make_async_copy(src.at[part], dst.at[part], sem.at[i, j]))
    for copy in copies:
        copy.start()
    for copy in copies:
        copy.wait()


def shards(dims, queries, key_rows, value_rows, cotangent, log_decay, norm_gain):
    ny, nz, nx, nhd = dims
    rows, width = queries.shape
    heads = log_decay.shape[0]
    piece = heads // nx
    chunks = piece * CUTS
    cut = DH // CUTS
    strip = cut // nz
    half = rows // 2
    vmem = pltpu.VMEM
    dma = pltpu.SemaphoreType.DMA
    most = max(nx, ny, nz) - 1
    scratch = [
        vmem((rows, width), BF16),
        vmem((rows, width), BF16),
        vmem((rows, width), BF16),
        vmem((rows, width), BF16),
        vmem((heads, rows), F32),
        vmem((1, width), F32),
        vmem((heads, rows, DH), F32),
        vmem((heads, rows), F32),
        vmem((rows, width), BF16),
        vmem((rows, width), BF16),
        vmem((rows, width), BF16),
        vmem((heads, 3, half, half), F32),
        vmem((heads, 3, half, half), BF16),
        vmem((rows, width), F32),
        vmem((rows, width), BF16),
        vmem((rows, width), F32),
        vmem((rows, width), F32),
        vmem((2, rows, DH), F32),
        vmem((2, chunks, nx, cut, DH), F32),
        vmem((2, chunks, nx, cut, DH), F32),
        vmem((2, chunks, cut, DH), F32),
        vmem((2, chunks, nz, strip, DH), F32),
        vmem((2, chunks, strip, DH), F32),
        vmem((2, chunks, ny, strip, DH), F32),
        vmem((2, chunks, nz, strip, DH), F32),
        vmem((2, chunks, cut, DH), F32),
        vmem((2, chunks, nx, cut, DH), F32),
        vmem((2, piece, nx, DH, DH), F32),
        vmem((nx, piece, 8, DH), F32),
        vmem((nx, piece, 8, DH), F32),
        vmem((piece, 8, DH), F32),
        vmem((nz, piece, 8, DH), F32),
        vmem((piece, 8, DH), F32),
        vmem((ny, piece, 8, DH), F32),
        vmem((8, rows), F32),
        vmem((nhd, 8, rows), F32),
        dma((2, 5, chunks)),
        dma((2, 5, chunks)),
        dma((3, most)),
        dma((3, most)),
        dma((max(nhd - 1, 1),)),
        dma((max(nhd - 1, 1),)),
        dma((6,)),
    ]
    grads = pl.pallas_call(
        functools.partial(kernel, dims),
        out_shape=[pltpu.VMEM((rows, width), BF16)] * 3,
        in_specs=[pl.BlockSpec(memory_space=pltpu.HBM)] * 6,
        out_specs=[pl.BlockSpec(memory_space=pltpu.VMEM)] * 3,
        scratch_shapes=scratch,
        compiler_params=pltpu.CompilerParams(
            collective_id=0, has_side_effects=True, vmem_limit_bytes=50 * 1024 * 1024
        ),
    )(*(
        pltpu.with_memory_space_constraint(array, pltpu.HBM)
        for array in (queries, key_rows, value_rows, cotangent, log_decay, norm_gain.reshape(1, width))
    ))
    return pl.pallas_call(
        hand_over,
        out_shape=[jax.ShapeDtypeStruct((rows, width), BF16)] * 3,
        in_specs=[pl.BlockSpec(memory_space=pl.ANY)] * 3,
        out_specs=[pl.BlockSpec(memory_space=pl.ANY)] * 3,
        scratch_shapes=[dma((3, SLICES))],
        compiler_params=pltpu.CompilerParams(vmem_limit_bytes=8 * 1024 * 1024),
    )(*grads)


def solution(mesh):
    ny, nz, nx = PARTS[mesh.shape["ctx"]]
    dims = (ny, nz, nx, mesh.shape["head"])
    in_specs = (
        P("ctx", "head"),
        P("ctx", "head"),
        P("ctx", "head"),
        P("ctx", "head"),
        P("head", "ctx"),
        P("head"),
    )
    out_specs = (P("ctx", "head"), P("ctx", "head"), P("ctx", "head"))
    return jax.shard_map(
        functools.partial(shards, dims), mesh=mesh, in_specs=in_specs, out_specs=out_specs, check_vma=False
    )
```

```python
import functools

import jax
import jax.numpy as jnp
from jax import lax
from jax.experimental import pallas as pl
from jax.experimental.pallas import tpu as pltpu
from jax.sharding import PartitionSpec as P

eps_norm = 1e-06
MESH = pl.DeviceIdType.MESH
F32, BF16 = jnp.float32, jnp.bfloat16
DH = 128
PARTS = {64: (4, 4, 4), 8: (2, 2, 2)}
X_OUT, Z_OUT, Y_ALL, Z_BACK, X_BACK = range(5)


def nn(a, b, **kw):
    return lax.dot_general(a, b, (((1,), (0,)), ((), ())), preferred_element_type=F32, **kw)


def nt(a, b, **kw):
    return lax.dot_general(a, b, (((1,), (1,)), ((), ())), preferred_element_type=F32, **kw)


def tn(a, b, **kw):
    return lax.dot_general(a, b, (((0,), (0,)), ((), ())), preferred_element_type=F32, **kw)


LATENCY = {"x": 3.5, "z": 4.0, "y": 3.5}
CARRY = {"x": 10.5, "z": 5.2, "y": 1.3}
FORWARD_US, BACKWARD_US, EVENT_US, SLACK_US = 0.22, 0.38, 0.2, 0.3
CUTS = 2


def timetable(chunks):
    free = {}
    events = []
    ready = [0.0] * chunks
    for level, axis in enumerate(["x", "z", "y", "z", "x"]):
        link = axis if level else "x"
        for c in range(chunks):
            begin = max(free.get(link, 0.0), ready[c])
            free[link] = begin + CARRY[axis] / chunks
            ready[c] = free[link] + LATENCY[axis]
            events.append((ready[c], level, c))
    return sorted(events)


def kernel(
    dims, q_in, k_in, v_in, cot_in, ld_in, gain_in, gq_ref, gk_ref, gv_ref,
    q_ref, k_ref, v_ref, cot_ref, ld_ref, gain_ref, cc, crow, kw, vw, qw, mask, sc, of, dob, gkf, gvf, stat,
    st, xr, tz, zr, uy, yr, ez, er, ex, fin,
    xds, xd, zds, zd, yds, yd, hs, hr,
    send_sem, recv_sem, dsend, drecv, hsend, hrecv, in_sem,
):
    ny, nz, nx, nhd = dims
    rows = q_ref.shape[0]
    half = rows // 2
    heads = ld_ref.shape[0]
    piece = heads // nx
    chunks = piece * CUTS
    cut = DH // CUTS
    strip = cut // nz
    exact = dict(precision=lax.Precision.HIGHEST)

    me = lax.axis_index("ctx")
    hd = lax.axis_index("head")
    x = lax.rem(me, nx)
    z = lax.rem(lax.div(me, nx), nz)
    y = lax.div(me, nx * nz)

    def x_at(i):
        return lax.rem(x + i, nx)

    def z_at(i):
        return lax.rem(z + i, nz)

    def y_at(i):
        return lax.rem(y + i, ny)

    def x_dev(i):
        return {"ctx": me - x + x_at(i), "head": hd}

    def z_dev(i):
        return {"ctx": me + (z_at(i) - z) * nx, "head": hd}

    def y_dev(i):
        return {"ctx": me + (y_at(i) - y) * (nx * nz), "head": hd}

    def h_dev(i):
        return {"ctx": me, "head": lax.rem(hd + i, nhd)}

    partners = (
        [x_dev(i) for i in range(1, nx)] + [z_dev(i) for i in range(1, nz)]
        + [y_dev(i) for i in range(1, ny)] + [h_dev(i) for i in range(1, nhd)]
    )
    barrier = pltpu.get_barrier_semaphore()
    for device in partners:
        pl.semaphore_signal(barrier, inc=1, device_id=device, device_id_type=MESH)

    def load(i, src, dst):
        copy = pltpu.make_async_copy(src, dst, in_sem.at[i])
        copy.start()
        return copy

    ld_load = load(0, ld_in, ld_ref)
    k_load = load(1, k_in, k_ref)
    v_load = load(2, v_in, v_ref)
    q_load = load(3, q_in, q_ref)
    cot_load = load(4, cot_in, cot_ref)
    gain_load = load(5, gain_in, gain_ref)

    def push(src, dst, send, recv, device):
        copy = pltpu.make_async_remote_copy(
            src_ref=src, dst_ref=dst, send_sem=send, recv_sem=recv, device_id=device, device_id_type=MESH
        )
        copy.start()
        return copy

    def columns(h):
        if isinstance(h, int):
            return pl.ds(h * DH, DH)
        return pl.ds(pl.multiple_of(h * DH, DH), DH)

    def order(count):
        return sorted(range(1, count), key=lambda i: -min(i, count - i))

    ld_load.wait()
    ld = ld_ref[...]
    r_i = lax.broadcasted_iota(jnp.int32, (rows, rows), 0)
    c_i = lax.broadcasted_iota(jnp.int32, (rows, rows), 1)
    cum_t = nt((r_i >= c_i).astype(F32), ld, **exact)
    end_t = cum_t[rows - 1:rows, :]
    bg_t = jnp.exp(end_t - cum_t)
    fall_t = jnp.exp(end_t)
    for h in range(heads):
        xds[h // piece, h % piece] = jnp.broadcast_to(fall_t[:, h:h + 1], (8, DH))

    xd[x] = xds[x]

    def x_send(way, c):
        for i in order(nx):
            push(
                st.at[way, c, x_at(i)], xr.at[way, c, x],
                send_sem.at[way, X_OUT, c], recv_sem.at[way, X_OUT, c], x_dev(i),
            )
        xr[way, c, x] = st[way, c, x]

    def arrive(way, level, c):
        size = sizes(level, way, c)
        pltpu.make_async_copy(size, size, recv_sem.at[way, level, c]).wait()

    def leave_behind(way):
        for level in range(5):
            for c in range(chunks):
                size = sizes(level, way, c)
                pltpu.make_async_copy(size, size, send_sem.at[way, level, c]).wait()

    def sizes(level, way, c):
        if level in (X_OUT, X_BACK):
            return xr.at[way, c, pl.ds(0, nx - 1)]
        return (zr if level in (Z_OUT, Z_BACK) else yr).at[way, c, pl.ds(0, (ny if level == Y_ALL else nz) - 1)]

    def along(way, count):
        return range(count) if way == 0 else range(count - 1, -1, -1)

    def keep(way, g, p, state):
        for u in range(CUTS):
            st[way, g * CUTS + u, p] = state[u * cut:(u + 1) * cut]

    k_load.wait()
    v_load.wait()
    decay_copies = {}
    for g in range(piece):
        for p in range(nx):
            h = p * piece + g
            back = jnp.broadcast_to(bg_t[:, h:h + 1], (rows, DH))
            weighted = (k_ref[:, columns(h)].astype(F32) * back).astype(BF16)
            kw[:, columns(h)] = weighted
            keep(0, g, p, tn(weighted, v_ref[:, columns(h)]))
        if g == 0:
            pl.semaphore_wait(barrier, len(partners))
            decay_copies[X_OUT] = [
                push(xds.at[x_at(i)], xd.at[x], dsend.at[0, i - 1], drecv.at[0, i - 1], x_dev(i)) for i in order(nx)
            ]
        for u in range(CUTS):
            x_send(0, g * CUTS + u)

    crow[...] = nn(ld, (r_i <= c_i).astype(F32), **exact)
    for h in range(heads):
        cc[h] = jnp.broadcast_to(cum_t[:, h:h + 1], (rows, DH))

    def z_decays():
        for copy in decay_copies[X_OUT]:
            copy.wait_recv()
        total = xd[0]
        for s in range(1, nx):
            total = total * xd[s]
        zds[...] = total
        zd[z] = total
        decay_copies[Z_OUT] = [
            push(zds, zd.at[z], dsend.at[1, i - 1], drecv.at[1, i - 1], z_dev(i)) for i in order(nz)
        ]

    def y_decays():
        for copy in decay_copies[Z_OUT]:
            copy.wait_recv()
        total = zd[0]
        for s in range(1, nz):
            total = total * zd[s]
        yds[...] = total
        yd[y] = total
        decay_copies[Y_ALL] = [
            push(yds, yd.at[y], dsend.at[2, i - 1], drecv.at[2, i - 1], y_dev(i)) for i in order(ny)
        ]

    def x_reduce(way, c):
        g = c // CUTS
        if way == 0 and c == 0:
            z_decays()
        arrive(way, X_OUT, c)
        path = list(along(way, nx))
        total = xr[way, c, path[0]]
        for s in path[1:]:
            total = xd[s, g, 0:1, :] * total + xr[way, c, s]
        tz[way, c] = total
        for i in order(nz):
            push(
                tz.at[way, c, pl.ds(z_at(i) * strip, strip)], zr.at[way, c, z],
                send_sem.at[way, Z_OUT, c], recv_sem.at[way, Z_OUT, c], z_dev(i),
            )
        zr[way, c, z] = tz[way, c, pl.ds(z * strip, strip)]

    def z_reduce(way, c):
        g = c // CUTS
        if way == 0 and c == 0:
            y_decays()
        arrive(way, Z_OUT, c)
        path = list(along(way, nz))
        total = zr[way, c, path[0]]
        for s in path[1:]:
            total = zd[s, g, 0:1, :] * total + zr[way, c, s]
        uy[way, c] = total
        for i in order(ny):
            push(
                uy.at[way, c], yr.at[way, c, y],
                send_sem.at[way, Y_ALL, c], recv_sem.at[way, Y_ALL, c], y_dev(i),
            )
        yr[way, c, y] = total

    def z_expand(way, c):
        g = c // CUTS
        if way == 0 and c == 0:
            for copy in decay_copies[Y_ALL]:
                copy.wait_recv()
        arrive(way, Y_ALL, c)
        state = jnp.zeros((strip, DH), F32)
        for s in along(way, ny):
            longer = yd[s, g, 0:1, :] * state + yr[way, c, s]
            before = (s < y) if way == 0 else (s > y)
            state = jnp.where(before, longer, state)
        for s in along(way, nz):
            ez[way, c, s] = state
            state = zd[s, g, 0:1, :] * state + zr[way, c, s]
        for i in order(nz):
            push(
                ez.at[way, c, z_at(i)], er.at[way, c, pl.ds(z * strip, strip)],
                send_sem.at[way, Z_BACK, c], recv_sem.at[way, Z_BACK, c], z_dev(i),
            )
        er[way, c, pl.ds(z * strip, strip)] = ez[way, c, z]

    def x_expand(way, c):
        g, u = c // CUTS, c % CUTS
        arrive(way, Z_BACK, c)
        state = er[way, c]
        for s in along(way, nx):
            ex[way, c, s] = state
            state = xd[s, g, 0:1, :] * state + xr[way, c, s]
        here = pl.ds(u * cut, cut)
        for i in order(nx):
            push(
                ex.at[way, c, x_at(i)], fin.at[way, g, x, here],
                send_sem.at[way, X_BACK, c], recv_sem.at[way, X_BACK, c], x_dev(i),
            )
        fin[way, g, x, here] = ex[way, c, x]

    def arrived(way, g):
        for u in range(CUTS):
            arrive(way, X_BACK, g * CUTS + u)

    def loop(count, body):
        pair = next(size for size in (4, 2, 1) if count % size == 0)

        def step(j, carry):
            for u in range(pair):
                body(j * pair + u)
            return carry

        lax.fori_loop(0, count // pair, step, 0)

    lower = (
        lax.broadcasted_iota(jnp.int32, (half, half), 0) >= lax.broadcasted_iota(jnp.int32, (half, half), 1)
    )

    def forward_work(h):
        here = columns(h)
        col = cc[h]
        line = crow[pl.ds(h, 1), :]
        m00 = jnp.where(lower, jnp.exp(jnp.minimum(col[:half] - line[:, :half], 0.0)), 0.0)
        m10 = jnp.exp(jnp.minimum(col[half:] - line[:, :half], 0.0))
        m11 = jnp.where(lower, jnp.exp(jnp.minimum(col[half:] - line[:, half:], 0.0)), 0.0)
        mask[h, 0], mask[h, 1], mask[h, 2] = m00, m10, m11
        q, k, v = q_ref[:, here], k_ref[:, here], v_ref[:, here]
        top = (nt(q[:half], k[:half]) * m00).astype(BF16)
        bottom = nt(q[half:], k)
        low_left = (bottom[:, :half] * m10).astype(BF16)
        low_right = (bottom[:, half:] * m11).astype(BF16)
        sc[h, 0], sc[h, 1], sc[h, 2] = top, low_left, low_right
        of[:half, here] = nn(top, v[:half])
        of[half:, here] = nn(low_left, v[:half]) + nn(low_right, v[half:])
        qw[:, here] = (q.astype(F32) * jnp.exp(col)).astype(BF16)
        vw[:, here] = (v.astype(F32) * jnp.exp(col[rows - 1:rows, :] - col)).astype(BF16)

    def enter(g):
        arrived(0, g)

        squares, inners = stat[0], stat[1]
        for p in range(nx):
            here = columns(p * piece + g)
            out = of[:, here] + nn(qw[:, here], fin[0, g, p].astype(BF16))
            of[:, here] = out
            squares += out * out
            inners += out * (gain_ref[:, here] * cot_ref[:, here].astype(F32))
        stat[0], stat[1] = squares, inners

    def backward_work(h):
        here = columns(h)
        d_out = dob[:, here]
        q, k, v = q_ref[:, here], k_ref[:, here], v_ref[:, here]
        top = (nt(d_out[:half], v[:half]) * mask[h, 0]).astype(BF16)
        bottom = nt(d_out[half:], v)
        low_left = (bottom[:, :half] * mask[h, 1]).astype(BF16)
        low_right = (bottom[:, half:] * mask[h, 2]).astype(BF16)
        entry = fin[0, lax.rem(h, piece), lax.div(h, piece)].astype(BF16)
        weighted = (d_out.astype(F32) * jnp.exp(cc[h])).astype(BF16)
        cross = nt(weighted, entry)
        gq_ref[:half, here] = (nn(top, k[:half]) + cross[:half]).astype(BF16)
        gq_ref[half:, here] = (nn(low_left, k[:half]) + nn(low_right, k[half:]) + cross[half:]).astype(BF16)
        gkf[:half, here] = tn(top, q[:half]) + tn(low_left, q[half:])
        gkf[half:, here] = tn(low_right, q[half:])
        gvf[:half, here] = tn(sc[h, 0], d_out[:half]) + tn(sc[h, 1], d_out[half:])
        gvf[half:, here] = tn(sc[h, 2], d_out[half:])

    def leave(g):
        arrived(1, g)

        def one(p):
            here = columns(p * piece + g)
            low = fin[1, g, p].astype(BF16)
            gk_ref[:, here] = (gkf[:, here] + nt(vw[:, here], low)).astype(BF16)
            gv_ref[:, here] = (gvf[:, here] + nn(kw[:, here], low)).astype(BF16)

        loop(nx, one)

    def scan(way, tasks, work, last):
        levels = [x_reduce, z_reduce, z_expand, x_expand]
        tasks = list(tasks)
        now = 0.0
        for when, level, c in timetable(chunks):
            if level < len(levels):
                while tasks and now + work <= when + SLACK_US:
                    tasks.pop(0)()
                    now += work
                levels[level](way, c)
                now = max(now, when) + EVENT_US
        for task in tasks:
            task()
        for g in range(piece):
            last(g)

    def some(work):
        return [functools.partial(loop, 2, lambda u, j=j: work(2 * j + u)) for j in range(heads // 2)]

    stat[...] = jnp.zeros_like(stat)
    q_load.wait()
    cot_load.wait()
    gain_load.wait()
    scan(0, some(forward_work), FORWARD_US * 2, enter)

    ones = jnp.ones((8, DH), F32)
    pick = lax.broadcasted_iota(jnp.int32, (8, rows), 0) < 4
    hs[...] = jnp.where(pick, nt(ones, stat[0], **exact), nt(ones, stat[1], **exact))
    hr[hd] = hs[...]
    h_copies = [push(hs, hr.at[hd], hsend.at[i - 1], hrecv.at[i - 1], h_dev(i)) for i in order(nhd)]
    for copy in h_copies:
        copy.wait_recv()
    both = hr[0]
    for s in range(1, nhd):
        both = both + hr[s]
    features = nhd * q_ref.shape[1]
    square_sum, inner_sum = both[0:1, :], both[4:5, :]
    root_mean = jnp.sqrt(square_sum / features + eps_norm)
    scales = jnp.where(pick, 1.0 / root_mean, inner_sum / (features * root_mean * root_mean * root_mean))
    where = lax.broadcasted_iota(jnp.int32, (8, DH), 0)
    stat[0] = tn(scales, (where == 0).astype(F32), **exact)
    stat[1] = tn(scales, (where == 4).astype(F32), **exact)

    for g in range(piece):
        def one(p, g=g):
            here = columns(p * piece + g)
            scaled = gain_ref[:, here] * cot_ref[:, here].astype(F32)
            d_out = (scaled * stat[0] - of[:, here] * stat[1]).astype(BF16)
            dob[:, here] = d_out
            keep(1, g, p, tn(qw[:, here], d_out))

        loop(nx, one)
        for u in range(CUTS):
            x_send(1, g * CUTS + u)

    def end(g):
        if g == 0:
            leave_behind(0)
            for level in decay_copies.values():
                for copy in level:
                    copy.wait_send()
            for copy in h_copies:
                copy.wait_send()
        leave(g)

    scan(1, some(backward_work), BACKWARD_US * 2, end)
    leave_behind(1)


SLICES = 4


def hand_over(a_in, b_in, c_in, a_out, b_out, c_out, sem):
    copies = []
    for i, (src, dst) in enumerate([(a_in, a_out), (b_in, b_out), (c_in, c_out)]):
        rows = src.shape[0] // SLICES
        for j in range(SLICES):
            part = pl.ds(j * rows, rows)
            copies.append(pltpu.make_async_copy(src.at[part], dst.at[part], sem.at[i, j]))
    for copy in copies:
        copy.start()
    for copy in copies:
        copy.wait()


def shards(dims, queries, key_rows, value_rows, cotangent, log_decay, norm_gain):
    ny, nz, nx, nhd = dims
    rows, width = queries.shape
    heads = log_decay.shape[0]
    piece = heads // nx
    chunks = piece * CUTS
    cut = DH // CUTS
    strip = cut // nz
    half = rows // 2
    vmem = pltpu.VMEM
    dma = pltpu.SemaphoreType.DMA
    most = max(nx, ny, nz) - 1
    scratch = [
        vmem((rows, width), BF16),
        vmem((rows, width), BF16),
        vmem((rows, width), BF16),
        vmem((rows, width), BF16),
        vmem((heads, rows), F32),
        vmem((1, width), F32),
        vmem((heads, rows, DH), F32),
        vmem((heads, rows), F32),
        vmem((rows, width), BF16),
        vmem((rows, width), BF16),
        vmem((rows, width), BF16),
        vmem((heads, 3, half, half), F32),
        vmem((heads, 3, half, half), BF16),
        vmem((rows, width), F32),
        vmem((rows, width), BF16),
        vmem((rows, width), F32),
        vmem((rows, width), F32),
        vmem((2, rows, DH), F32),
        vmem((2, chunks, nx, cut, DH), F32),
        vmem((2, chunks, nx, cut, DH), F32),
        vmem((2, chunks, cut, DH), F32),
        vmem((2, chunks, nz, strip, DH), F32),
        vmem((2, chunks, strip, DH), F32),
        vmem((2, chunks, ny, strip, DH), F32),
        vmem((2, chunks, nz, strip, DH), F32),
        vmem((2, chunks, cut, DH), F32),
        vmem((2, chunks, nx, cut, DH), F32),
        vmem((2, piece, nx, DH, DH), F32),
        vmem((nx, piece, 8, DH), F32),
        vmem((nx, piece, 8, DH), F32),
        vmem((piece, 8, DH), F32),
        vmem((nz, piece, 8, DH), F32),
        vmem((piece, 8, DH), F32),
        vmem((ny, piece, 8, DH), F32),
        vmem((8, rows), F32),
        vmem((nhd, 8, rows), F32),
        dma((2, 5, chunks)),
        dma((2, 5, chunks)),
        dma((3, most)),
        dma((3, most)),
        dma((max(nhd - 1, 1),)),
        dma((max(nhd - 1, 1),)),
        dma((6,)),
    ]
    grads = pl.pallas_call(
        functools.partial(kernel, dims),
        out_shape=[pltpu.VMEM((rows, width), BF16)] * 3,
        in_specs=[pl.BlockSpec(memory_space=pltpu.HBM)] * 6,
        out_specs=[pl.BlockSpec(memory_space=pltpu.VMEM)] * 3,
        scratch_shapes=scratch,
        compiler_params=pltpu.CompilerParams(
            collective_id=0, has_side_effects=True, vmem_limit_bytes=50 * 1024 * 1024
        ),
    )(*(
        pltpu.with_memory_space_constraint(array, pltpu.HBM)
        for array in (queries, key_rows, value_rows, cotangent, log_decay, norm_gain.reshape(1, width))
    ))
    return pl.pallas_call(
        hand_over,
        out_shape=[jax.ShapeDtypeStruct((rows, width), BF16)] * 3,
        in_specs=[pl.BlockSpec(memory_space=pl.ANY)] * 3,
        out_specs=[pl.BlockSpec(memory_space=pl.ANY)] * 3,
        scratch_shapes=[dma((3, SLICES))],
        compiler_params=pltpu.CompilerParams(vmem_limit_bytes=8 * 1024 * 1024),
    )(*grads)


def solution(mesh):
    ny, nz, nx = PARTS[mesh.shape["ctx"]]
    dims = (ny, nz, nx, mesh.shape["head"])
    in_specs = (
        P("ctx", "head"),
        P("ctx", "head"),
        P("ctx", "head"),
        P("ctx", "head"),
        P("head", "ctx"),
        P("head"),
    )
    out_specs = (P("ctx", "head"), P("ctx", "head"), P("ctx", "head"))
    return jax.shard_map(
        functools.partial(shards, dims), mesh=mesh, in_specs=in_specs, out_specs=out_specs, check_vma=False
    )
```
